32 devices in a mesh: tensor: 4 (over z), row: 2 (over core), col: 4 (over y, x).
Axes of the slice: x: 2, y: 2, z: 4, core: 2. Of those that a mesh axis runs over, the one named last changes fastest.
Arguments:
- features: bfloat16 [1024, 6144], P(('row', 'col'), 'tensor'), may hold values from -8 to 8
- w_proj: bfloat16 [6144, 1024], P('tensor'), may hold values from -0.078125 to 0.078125
- flags: int32 [1024], P(('row', 'col')), may hold values 0 or 1
- rates: float32 [5], replicated, may hold values from 0.25 to 4
Outputs:
- feature_grad: bfloat16 [1024, 6144], P(('row', 'col'), 'tensor')
The draws below stay inside these ranges and needn't reach their ends.
All inputs are finite; a program needn't handle non-finite values. No bound on the sum of `flags` on one device may be relied on, other than what follows from the above.
Results may differ from the reference program's by a relative error of at most 0.029.
Values may be sent and summed in bfloat16 or wider, within the bound.
A program may use at most 64 MiB of HBM per device.

```python
import math
import jax
import jax.numpy as jnp
from jax import lax

D = 6144
P_SIZE = 1024
NB = 5
GROUP_ROWS = 128
NROWS = 1024
N_TENSOR = 4
N_ROW = 2
N_COL = 4


def draw_features(key, part):
    key = jax.random.fold_in(key, 11)
    key_ids, key_centre, key_noise, key_scale = jax.random.split(key, 4)
    labels = jax.random.randint(key_ids, (NROWS,), 0, 16)
    centres = jax.random.normal(key_centre, (16, D), jnp.float32)
    noise = jax.random.normal(key_noise, (NROWS, D), jnp.float32)
    scale = jnp.exp(jax.random.uniform(key_scale, (NROWS, 1), jnp.float32, -0.35, 0.35))
    values = scale * (0.8 * centres[labels] + 0.6 * noise)
    return jnp.clip(values, -8.0, 8.0).astype(jnp.bfloat16)


def plant(entries, own_key, smallest, largest):
    dims = entries.shape
    place = [jax.random.randint(jax.random.fold_in(own_key, axis), (), 0, dims[axis]) for axis in range(len(dims))]
    entries = entries.at[tuple(place)].set(smallest)
    longest = dims.index(max(dims))
    place[longest] = (place[longest] + 1) % dims[longest]
    return entries.at[tuple(place)].set(largest)


def steps_of(own_key, extent, shards, low, top_value):
    gain, own = 1.0, jax.random.fold_in(own_key, 6)
    for axis_at, shards_of in shards:
        draws = jnp.exp(jax.random.uniform(jax.random.fold_in(own, axis_at), (shards_of,), jnp.float32, low / len(shards), top_value / len(shards)))
        gain = gain * jnp.repeat(draws, extent[axis_at] // shards_of).reshape([-1 if axis == axis_at else 1 for axis in range(len(extent))])
    return gain


def normal_values(stream_key, extent, scale, bound, pieces=(), kind=jnp.bfloat16):
    array = scale * jax.random.normal(stream_key, extent, jnp.float32)
    if pieces:
        array = array * steps_of(stream_key, extent, pieces, -0.22, 0.18)
    return jnp.clip(array, -bound, bound).astype(kind)


def setup_inputs(seed: int = 0) -> dict:
    arg_keys = jax.random.split(jax.random.key(seed), 5)
    return {
        "features": draw_features(jax.random.fold_in(arg_keys[4], 71), 0),
        "w_proj": normal_values(arg_keys[1], (D, P_SIZE), D ** -0.5, 0.078125, ((0, 4),)),
        "flags": plant((jax.random.randint(arg_keys[2], (NROWS,), 0, 2) < 1).astype(jnp.int32), jax.random.fold_in(arg_keys[2], 1), 0, 1),
        "rates": jnp.clip(jnp.exp(jax.random.uniform(arg_keys[3], (NB,), jnp.float32, math.log(0.25), math.log(4.0))), 0.25, 4.0),
    }


def pair_terms(row_z, row_s, col_z, col_s, rates):
    hp = lax.Precision.HIGHEST
    row_norm = jnp.sum(row_z * row_z, axis=1)
    col_norm = jnp.sum(col_z * col_z, axis=1)
    cross = jnp.dot(row_z, col_z.T, precision=hp)
    dist = jnp.maximum(row_norm[:, None] + col_norm[None, :] - 2.0 * cross, 0.0) / P_SIZE
    kernel = jnp.zeros_like(dist)
    for band in range(NB):
        kernel = kernel + rates[band] * jnp.exp(-rates[band] * dist)
    mixed = (-16.0 / P_SIZE) * row_s[:, None] * col_s[None, :] * kernel
    rounded = mixed.astype(jnp.bfloat16).astype(jnp.float32)
    row_part = jnp.sum(mixed, axis=1)[:, None] * row_z - jnp.dot(rounded, col_z, precision=hp)
    col_part = jnp.sum(mixed, axis=0)[:, None] * col_z - jnp.dot(rounded.T, row_z, precision=hp)
    row_part = row_part.astype(jnp.bfloat16).astype(jnp.float32)
    col_part = col_part.astype(jnp.bfloat16).astype(jnp.float32)
    return row_part, col_part


def reference(features, w_proj, flags, rates):
    hp = lax.Precision.HIGHEST
    n_row = N_ROW
    n_col = N_COL
    n_ten = N_TENSOR
    group = GROUP_ROWS
    quarter = group // n_ten
    weights = w_proj.astype(jnp.float32)
    proj = jnp.dot(features.astype(jnp.float32), weights, precision=hp)
    proj = proj.astype(jnp.bfloat16).astype(jnp.float32)
    signs = (1 - 2 * flags).astype(jnp.float32)
    grid_z = proj.reshape(n_row, n_col, group, P_SIZE)
    grid_s = signs.reshape(n_row, n_col, group)
    zero = jnp.int32(0)

    def one_tile(accum, index):
        rpos = (index // (n_col * n_ten)).astype(jnp.int32)
        cpos = ((index // n_ten) % n_col).astype(jnp.int32)
        tpos = (index % n_ten).astype(jnp.int32)
        start = (tpos * quarter).astype(jnp.int32)
        row_z = lax.dynamic_slice(grid_z, (zero, cpos, zero, zero), (n_row, 1, group, P_SIZE)).reshape(n_row * group, P_SIZE)
        row_s = lax.dynamic_slice(grid_s, (zero, cpos, zero), (n_row, 1, group)).reshape(n_row * group)
        col_z = lax.dynamic_slice(grid_z, (rpos, zero, start, zero), (1, n_col, quarter, P_SIZE)).reshape(n_col * quarter, P_SIZE)
        col_s = lax.dynamic_slice(grid_s, (rpos, zero, start), (1, n_col, quarter)).reshape(n_col * quarter)
        row_part, col_part = pair_terms(row_z, row_s, col_z, col_s, rates)
        old = lax.dynamic_slice(accum, (zero, cpos, zero, zero), (n_row, 1, group, P_SIZE))
        accum = lax.dynamic_update_slice(accum, old + row_part.reshape(n_row, 1, group, P_SIZE), (zero, cpos, zero, zero))
        old = lax.dynamic_slice(accum, (rpos, zero, start, zero), (1, n_col, quarter, P_SIZE))
        accum = lax.dynamic_update_slice(accum, old + col_part.reshape(1, n_col, quarter, P_SIZE), (rpos, zero, start, zero))
        return accum, None

    accum = jnp.zeros((n_row, n_col, group, P_SIZE), jnp.float32)
    accum, _ = lax.scan(one_tile, accum, jnp.arange(n_row * n_col * n_ten, dtype=jnp.int32))
    grad_z = accum.reshape(n_row * n_col * group, P_SIZE).astype(jnp.bfloat16).astype(jnp.float32)
    result = jnp.dot(grad_z, weights.T, precision=hp)
    return result.astype(jnp.bfloat16)
```

```python
import functools
import jax
import jax.numpy as jnp
from jax import lax
from jax.experimental import pallas as pl
from jax.experimental.pallas import tpu as pltpu
from jax.sharding import PartitionSpec as P

MESH = pl.DeviceIdType.MESH
PARTS = 2
NT_DIMS = (((1,), (1,)), ((), ()))


def kernel(
    n_tensor, n_row, n_col, n_rates,
    f_hbm, w_hbm, flags_ref, rates_ref, out_ref,
    f_ref, w_ref, part_ref, mine_ref, rs_ref, z_ref, s_ref, acc_ref, sum_ref,
    load_sem, rs_send, rs_recv, t_send, t_recv, c_send, c_recv, r_send, r_recv, s_send, s_recv,
):
    t, r, c = lax.axis_index("tensor"), lax.axis_index("row"), lax.axis_index("col")
    group = f_ref.shape[0]
    quarter = group // n_tensor
    depth, wide = w_ref.shape[1], w_ref.shape[2]
    width = wide * PARTS
    bits = [1 << b for b in range(n_col.bit_length() - 1)]

    def base(col, row):
        return pl.multiple_of((col * n_row + row) * group, group)

    def block(h, col, row, tpos):
        start = pl.multiple_of((col * n_row + row) * group + tpos * quarter, quarter)
        return z_ref.at[h, pl.ds(start, quarter), :]

    sends = []

    def push(src, dst, send, recv, **to):
        copy = pltpu.make_async_remote_copy(
            src_ref=src, dst_ref=dst, send_sem=send, recv_sem=recv, device_id=to, device_id_type=MESH
        )
        copy.start()
        sends.append(copy)

    def arrived(dst, recv):
        pltpu.make_async_copy(dst, dst, recv).wait()

    loads = [pltpu.make_async_copy(f_hbm, f_ref, load_sem.at[PARTS])]
    for h in range(PARTS):
        loads.append(
            pltpu.make_async_copy(w_hbm.at[:, pl.ds(h * wide, wide)], w_ref.at[h], load_sem.at[h])
        )
    for load in loads:
        load.start()

    barrier = pltpu.get_barrier_semaphore()
    near = [(dr, dc) for dr in range(n_row) for dc in range(n_col) if (dr, dc) != (0, 0)]
    for k in range(1, n_tensor):
        pl.semaphore_signal(
            barrier, inc=1, device_id={"tensor": lax.rem(t + k, n_tensor)}, device_id_type=MESH
        )
    for dr, dc in near:
        pl.semaphore_signal(
            barrier,
            inc=1,
            device_id={"row": lax.rem(r + dr, n_row), "col": lax.rem(c + dc, n_col)},
            device_id_type=MESH,
        )

    s_ref[c * n_row + r] = jnp.broadcast_to(
        (1 - 2 * flags_ref[...]).astype(jnp.float32), s_ref.shape[1:]
    )
    acc_ref[...] = jnp.zeros_like(acc_ref)
    sum_ref[...] = jnp.zeros_like(sum_ref)

    loads[0].wait()
    for h in range(PARTS):
        loads[1 + h].wait()
        partial = jnp.dot(f_ref[...], w_ref[h], preferred_element_type=jnp.float32)
        part_ref[h] = partial.astype(jnp.bfloat16)
        mine_ref[...] = partial
        if h == 0:
            pl.semaphore_wait(barrier, n_tensor - 1 + len(near))
        for k in range(1, n_tensor):
            peer = lax.rem(t + k, n_tensor)
            rows = pl.ds(pl.multiple_of(peer * quarter, quarter), quarter)
            push(
                part_ref.at[h, rows, :], rs_ref.at[h, k - 1],
                rs_send.at[h, k - 1], rs_recv.at[h, k - 1], tensor=peer,
            )
        own = mine_ref[pl.ds(pl.multiple_of(t * quarter, quarter), quarter), :]
        acc_ref[h, 0:quarter, :] = own
    for index, (dr, dc) in enumerate(near):
        push(
            s_ref.at[c * n_row + r], s_ref.at[c * n_row + r], s_send.at[index], s_recv.at[index],
            row=lax.rem(r + dr, n_row), col=lax.rem(c + dc, n_col),
        )

    order = [bits if h % 2 == 0 else bits[::-1] for h in range(PARTS)]

    def to_cols(h, k, mask, step):
        for j in range(step, len(bits)):
            tpos = lax.rem(t - k + n_tensor, n_tensor)
            src = block(h, jnp.bitwise_xor(c, mask), r, tpos)
            got = mask ^ order[h][j]
            push(
                src, src, c_send.at[h, k, got], c_recv.at[h, k, got],
                col=jnp.bitwise_xor(c, order[h][j]),
            )

    def to_rows(h, mask):
        src = z_ref.at[h, pl.ds(base(jnp.bitwise_xor(c, mask), r), group), :]
        for k in range(1, n_row):
            push(
                src, src, r_send.at[h, mask, k - 1], r_recv.at[h, mask, k - 1],
                row=lax.rem(r + k, n_row),
            )

    for h in range(PARTS):
        total = acc_ref[h, 0:quarter, :]
        for k in range(1, n_tensor):
            arrived(rs_ref.at[h, k - 1], rs_recv.at[h, k - 1])
            total = total + rs_ref[h, k - 1].astype(jnp.float32)
        start = pl.multiple_of((c * n_row + r) * group + t * quarter, quarter)
        z_ref[h, pl.ds(start, quarter), :] = total.astype(jnp.bfloat16)
        for k in range(1, n_tensor):
            src = block(h, c, r, t)
            push(
                src, src, t_send.at[h, k - 1], t_recv.at[h, k - 1], tensor=lax.rem(t + k, n_tensor)
            )
        to_cols(h, 0, 0, 0)
    for k in range(1, n_tensor):
        for h in range(PARTS):
            tpos = lax.rem(t - k + n_tensor, n_tensor)
            arrived(block(h, c, r, tpos), t_recv.at[h, k - 1])
            to_cols(h, k, 0, 0)
    for h in range(PARTS):
        to_rows(h, 0)

    acc_ref[...] = jnp.zeros_like(acc_ref)
    for index, (dr, dc) in enumerate(near):
        from_r, from_c = lax.rem(r - dr + n_row, n_row), lax.rem(c - dc + n_col, n_col)
        arrived(s_ref.at[from_c * n_row + from_r], s_recv.at[index])

    own_rows = pl.ds(base(c, r), group)
    own_norm = jnp.zeros((group, 1), jnp.float32)
    for h in range(PARTS):
        own_norm += jnp.sum(jnp.square(z_ref[h, own_rows, :].astype(jnp.float32)), axis=1, keepdims=True)

    def pairs(col, row, count):
        rows = pl.ds(base(col, row), count * group)
        cross = jnp.zeros((group, count * group), jnp.float32)
        norm = jnp.zeros((count * group, 1), jnp.float32)
        for h in range(PARTS):
            other = z_ref[h, rows, :]
            norm += jnp.sum(jnp.square(other.astype(jnp.float32)), axis=1, keepdims=True)
            cross += lax.dot_general(
                z_ref[h, own_rows, :], other, NT_DIMS, preferred_element_type=jnp.float32
            )
        norm = jnp.transpose(jnp.broadcast_to(norm, (count * group, 128)))[0:1, :]
        sign = jnp.concatenate([s_ref[col * n_row + row + i][0:1, :] for i in range(count)], axis=1)
        dist = jnp.maximum(own_norm + norm - 2.0 * cross, 0.0) * (1.0 / width)
        mixed = jnp.zeros_like(dist)
        for band in range(n_rates):
            mixed = mixed + rates_ref[band] * jnp.exp(-rates_ref[band] * dist)
        mixed = mixed * sign
        sum_ref[...] += jnp.sum(mixed, axis=1, keepdims=True)
        rounded = mixed.astype(jnp.bfloat16)
        for h in range(PARTS):
            acc_ref[h] += jnp.dot(rounded, z_ref[h, rows, :], preferred_element_type=jnp.float32)

    def column(mask):
        col = jnp.bitwise_xor(c, mask)
        for h in range(PARTS):
            for k in range(1, n_row):
                from_r = lax.rem(r - k + n_row, n_row)
                arrived(
                    z_ref.at[h, pl.ds(base(col, from_r), group), :], r_recv.at[h, mask, k - 1]
                )
        count = 2 if n_row % 2 == 0 else 1
        if n_row <= 2:
            pairs(col, 0, count)
        else:
            pl.loop(0, n_row // count)(lambda i: pairs(col, i * count, count))

    for step in range(len(bits)):
        masks = [[0] for _ in range(PARTS)]
        for h in range(PARTS):
            for j in range(step):
                masks[h] = masks[h] + [m ^ order[h][j] for m in masks[h]]
        for place in range(len(masks[0])):
            for k in range(n_tensor):
                for h in range(PARTS):
                    mask = masks[h][place] ^ order[h][step]
                    tpos = lax.rem(t - k + n_tensor, n_tensor)
                    arrived(block(h, jnp.bitwise_xor(c, mask), r, tpos), c_recv.at[h, k, mask])
                    to_cols(h, k, mask, step + 1)
            for h in range(PARTS):
                to_rows(h, masks[h][place] ^ order[h][step])
        if step == 0:
            column(0)
    for mask in range(1, n_col):
        column(mask)

    lead = jnp.transpose(jnp.broadcast_to(s_ref[c * n_row + r][0:1, :], (128, group)))[:, 0:1]
    lead = lead * (-32.0 / width)
    grads = []
    for h in range(PARTS):
        own = z_ref[h, own_rows, :].astype(jnp.float32)
        grads.append((lead * (sum_ref[...] * own - acc_ref[h])).astype(jnp.bfloat16))
    tile = 512
    for at in range(0, depth, tile):
        result = jnp.zeros((group, tile), jnp.float32)
        for h in range(PARTS):
            result += lax.dot_general(
                grads[h], w_ref[h, at : at + tile, :], NT_DIMS, preferred_element_type=jnp.float32
            )
        out_ref[:, at : at + tile] = result.astype(jnp.bfloat16)
    for copy in sends:
        copy.wait_send()


def shards(features, w_proj, flags, rates):
    n_tensor, n_row, n_col = (lax.axis_size(name) for name in ("tensor", "row", "col"))
    group, depth = features.shape
    width = w_proj.shape[1]
    wide = width // PARTS
    quarter = group // n_tensor
    rows = group * n_row * n_col
    near = n_row * n_col - 1
    dma = pltpu.SemaphoreType.DMA
    return pl.pallas_call(
        functools.partial(kernel, n_tensor, n_row, n_col, rates.shape[0]),
        out_shape=jax.ShapeDtypeStruct((group, depth), jnp.bfloat16),
        in_specs=[
            pl.BlockSpec(memory_space=pl.ANY),
            pl.BlockSpec(memory_space=pl.ANY),
            pl.BlockSpec(memory_space=pltpu.VMEM),
            pl.BlockSpec(memory_space=pltpu.SMEM),
        ],
        out_specs=pl.BlockSpec(memory_space=pltpu.VMEM),
        scratch_shapes=[
            pltpu.VMEM((group, depth), jnp.bfloat16),
            pltpu.VMEM((PARTS, depth, wide), jnp.bfloat16),
            pltpu.VMEM((PARTS, group, wide), jnp.bfloat16),
            pltpu.VMEM((group, wide), jnp.float32),
            pltpu.VMEM((PARTS, n_tensor - 1, quarter, wide), jnp.bfloat16),
            pltpu.VMEM((PARTS, rows, wide), jnp.bfloat16),
            pltpu.VMEM((n_row * n_col, 8, group), jnp.float32),
            pltpu.VMEM((PARTS, group, wide), jnp.float32),
            pltpu.VMEM((group, 1), jnp.float32),
            dma((PARTS + 1,)),
            dma((PARTS, n_tensor - 1)),
            dma((PARTS, n_tensor - 1)),
            dma((PARTS, n_tensor - 1)),
            dma((PARTS, n_tensor - 1)),
            dma((PARTS, n_tensor, n_col)),
            dma((PARTS, n_tensor, n_col)),
            dma((PARTS, n_col, n_row - 1)),
            dma((PARTS, n_col, n_row - 1)),
            dma((near,)),
            dma((near,)),
        ],
        compiler_params=pltpu.CompilerParams(
            collective_id=0, has_side_effects=True, vmem_limit_bytes=56 * 1024 * 1024
        ),
        cost_estimate=pl.CostEstimate(
            flops=4 * group * depth * width + 4 * group * rows * width,
            bytes_accessed=2 * (depth * width + 2 * group * depth),
            transcendentals=rates.shape[0] * group * rows,
        ),
        name="mmd",
    )(features, w_proj, flags.reshape(1, group), rates)


def solution(mesh):
    in_specs = (P(("row", "col"), "tensor"), P("tensor", None), P(("row", "col")), P())
    out_specs = P(("row", "col"), "tensor")
    return jax.shard_map(shards, mesh=mesh, in_specs=in_specs, out_specs=out_specs, check_vma=False)
```

```python
import functools
import jax
import jax.numpy as jnp
from jax import lax
from jax.experimental import pallas as pl
from jax.experimental.pallas import tpu as pltpu
from jax.sharding import PartitionSpec as P

MESH = pl.DeviceIdType.MESH
PARTS = 4
NT_DIMS = (((1,), (1,)), ((), ()))


def kernel(
    n_tensor, n_row, n_col, n_rates,
    f_hbm, w_hbm, flags_ref, rates_ref, out_ref,
    f_ref, w_ref, part_ref, rs_ref, z_ref, s_ref, acc_ref, sum_ref,
    load_sem, rs_send, rs_recv, t_send, t_recv, c_send, c_recv, r_send, r_recv, s_send, s_recv,
):
    t, r, c = lax.axis_index("tensor"), lax.axis_index("row"), lax.axis_index("col")
    group = f_ref.shape[0]
    quarter = group // n_tensor
    depth, wide = w_ref.shape[1], w_ref.shape[2]
    width = wide * PARTS
    bits = [1 << b for b in range(n_col.bit_length() - 1)]

    def base(col, row):
        return pl.multiple_of((col * n_row + row) * group, group)

    def block(h, col, row, tpos):
        start = pl.multiple_of((col * n_row + row) * group + tpos * quarter, quarter)
        return z_ref.at[h, pl.ds(start, quarter), :]

    sends = []

    def push(src, dst, send, recv, **to):
        copy = pltpu.make_async_remote_copy(
            src_ref=src, dst_ref=dst, send_sem=send, recv_sem=recv, device_id=to, device_id_type=MESH
        )
        copy.start()
        sends.append(copy)

    def arrived(dst, recv):
        pltpu.make_async_copy(dst, dst, recv).wait()

    loads = [pltpu.make_async_copy(f_hbm, f_ref, load_sem.at[PARTS])]
    for h in range(PARTS):
        loads.append(
            pltpu.make_async_copy(w_hbm.at[:, pl.ds(h * wide, wide)], w_ref.at[h], load_sem.at[h])
        )
    for load in loads:
        load.start()

    barrier = pltpu.get_barrier_semaphore()
    near = [(dr, dc) for dr in range(n_row) for dc in range(n_col) if (dr, dc) != (0, 0)]
    for k in range(1, n_tensor):
        pl.semaphore_signal(
            barrier, inc=1, device_id={"tensor": lax.rem(t + k, n_tensor)}, device_id_type=MESH
        )
    for dr, dc in near:
        pl.semaphore_signal(
            barrier,
            inc=1,
            device_id={"row": lax.rem(r + dr, n_row), "col": lax.rem(c + dc, n_col)},
            device_id_type=MESH,
        )

    s_ref[c * n_row + r] = jnp.broadcast_to(
        (1 - 2 * flags_ref[...]).astype(jnp.float32), s_ref.shape[1:]
    )
    order = [bits if h % 2 == 0 else bits[::-1] for h in range(PARTS)]
    hops = []
    for j in range(n_tensor - 1):
        k = jnp.int32(0)
        for at in range(n_tensor):
            nearest = sorted((x for x in range(n_tensor) if x != at), key=lambda x: (abs(x - at), x))
            k = k + jnp.where(t == at, (at - nearest[j]) % n_tensor, 0)
        hops.append(k)
    ks = [0] + hops

    def of(k):
        return lax.rem(t - k + n_tensor, n_tensor)

    def to_cols(h, k, mask, step):
        for j in range(step, len(bits)):
            src = block(h, jnp.bitwise_xor(c, mask), r, of(k))
            got = mask ^ order[h][j]
            push(
                src, src, c_send.at[h, k, got], c_recv.at[h, k, got],
                col=jnp.bitwise_xor(c, order[h][j]),
            )

    def to_rows(h, mask):
        src = z_ref.at[h, pl.ds(base(jnp.bitwise_xor(c, mask), r), group), :]
        for k in range(1, n_row):
            push(
                src, src, r_send.at[h, mask, k - 1], r_recv.at[h, mask, k - 1],
                row=lax.rem(r + k, n_row),
            )

    def project(h):
        loads[1 + h].wait()
        partial = jnp.dot(f_ref[...], w_ref[h], preferred_element_type=jnp.float32)
        part_ref[h] = partial.astype(jnp.bfloat16)
        acc_ref[h] = partial
        if h == 0:
            pl.semaphore_wait(barrier, n_tensor - 1 + len(near))
        for k in range(1, n_tensor):
            peer = lax.rem(t + k, n_tensor)
            rows = pl.ds(pl.multiple_of(peer * quarter, quarter), quarter)
            push(
                part_ref.at[h, rows, :], rs_ref.at[h, k - 1],
                rs_send.at[h, k - 1], rs_recv.at[h, k - 1], tensor=peer,
            )

    def line(h, k, right, left):
        src = block(h, c, r, of(k))
        for index, (cond, near_k, there) in enumerate(
            ((right, lax.rem(k + 1, n_tensor), t + 1), (left, lax.rem(k - 1 + n_tensor, n_tensor), t - 1))
        ):
            slot = jnp.maximum(near_k - 1, 0)
            copy = pltpu.make_async_remote_copy(
                src_ref=src, dst_ref=src, send_sem=t_send.at[h, k, index], recv_sem=t_recv.at[h, slot],
                device_id={"tensor": lax.rem(there + n_tensor, n_tensor)}, device_id_type=MESH,
            )
            pl.when(cond)(copy.start)
            lines.append((cond, copy))

    lines = []

    def combine(h):
        total = acc_ref[h, pl.ds(pl.multiple_of(t * quarter, quarter), quarter), :]
        for k in range(1, n_tensor):
            arrived(rs_ref.at[h, k - 1], rs_recv.at[h, k - 1])
            total = total + rs_ref[h, k - 1].astype(jnp.float32)
        start = pl.multiple_of((c * n_row + r) * group + t * quarter, quarter)
        z_ref[h, pl.ds(start, quarter), :] = total.astype(jnp.bfloat16)
        line(h, 0, t < n_tensor - 1, t > 0)
        to_cols(h, 0, 0, 0)

    def gather_line(h):
        for k in hops:
            arrived(block(h, c, r, of(k)), t_recv.at[h, k - 1])
            line(h, k, (t >= k) & (t < n_tensor - 1), (t < k) & (t > 0))
            to_cols(h, k, 0, 0)
        to_rows(h, 0)

    def gather_cols(h, step, mask):
        for k in ks:
            arrived(block(h, jnp.bitwise_xor(c, mask), r, of(k)), c_recv.at[h, k, mask])
            to_cols(h, k, mask, step + 1)
        to_rows(h, mask)

    loads[0].wait()
    for s in range(PARTS + 4):
        if s < PARTS:
            project(s)
        if s == 0:
            for index, (dr, dc) in enumerate(near):
                push(
                    s_ref.at[c * n_row + r], s_ref.at[c * n_row + r], s_send.at[index], s_recv.at[index],
                    row=lax.rem(r + dr, n_row), col=lax.rem(c + dc, n_col),
                )
        if 0 <= s - 3 < PARTS:
            gather_line(s - 3)
        if 0 <= s - 1 < PARTS:
            combine(s - 1)
        if bits and 0 <= s - 4 < PARTS:
            gather_cols(s - 4, 0, order[s - 4][0])

    acc_ref[...] = jnp.zeros_like(acc_ref)
    sum_ref[...] = jnp.zeros_like(sum_ref)
    for index, (dr, dc) in enumerate(near):
        from_r, from_c = lax.rem(r - dr + n_row, n_row), lax.rem(c - dc + n_col, n_col)
        arrived(s_ref.at[from_c * n_row + from_r], s_recv.at[index])

    def own_norms():
        norm = jnp.zeros((group, 1), jnp.float32)
        for h in range(PARTS):
            norm += jnp.sum(jnp.square(z_ref[h, own_rows, :].astype(jnp.float32)), axis=1, keepdims=True)
        return norm

    own_rows = pl.ds(base(c, r), group)
    own_norm = own_norms()

    def pairs(col, row, count):
        rows = pl.ds(base(col, row), count * group)
        cross = jnp.zeros((group, count * group), jnp.float32)
        norm = jnp.zeros((count * group, 1), jnp.float32)
        for h in range(PARTS):
            other = z_ref[h, rows, :]
            norm += jnp.sum(jnp.square(other.astype(jnp.float32)), axis=1, keepdims=True)
            cross += lax.dot_general(
                z_ref[h, own_rows, :], other, NT_DIMS, preferred_element_type=jnp.float32
            )
        norm = jnp.transpose(jnp.broadcast_to(norm, (count * group, 128)))[0:1, :]
        sign = jnp.concatenate([s_ref[col * n_row + row + i][0:1, :] for i in range(count)], axis=1)
        dist = jnp.maximum(own_norm + norm - 2.0 * cross, 0.0) * (1.0 / width)
        mixed = jnp.zeros_like(dist)
        for band in range(n_rates):
            mixed = mixed + rates_ref[band] * jnp.exp(-rates_ref[band] * dist)
        mixed = mixed * sign
        sum_ref[...] += jnp.sum(mixed, axis=1, keepdims=True)
        rounded = mixed.astype(jnp.bfloat16)
        for h in range(PARTS):
            acc_ref[h] += jnp.dot(rounded, z_ref[h, rows, :], preferred_element_type=jnp.float32)

    def column(mask):
        col = jnp.bitwise_xor(c, mask)
        for h in range(PARTS):
            for k in range(1, n_row):
                from_r = lax.rem(r - k + n_row, n_row)
                arrived(
                    z_ref.at[h, pl.ds(base(col, from_r), group), :], r_recv.at[h, mask, k - 1]
                )
        count = 2 if n_row % 2 == 0 else 1
        if n_row <= 2:
            pairs(col, 0, count)
        else:
            pl.loop(0, n_row // count)(lambda i: pairs(col, i * count, count))

    arrived_parts = {0: PARTS}
    ready, finished = [0], []

    def note(mask):
        arrived_parts[mask] = arrived_parts.get(mask, 0) + 1
        if arrived_parts[mask] == PARTS:
            finished.append(mask)

    for h in range(PARTS):
        if bits:
            note(order[h][0])
    for step in range(1, len(bits)):
        masks = [[0] for _ in range(PARTS)]
        for h in range(PARTS):
            for j in range(step):
                masks[h] = masks[h] + [m ^ order[h][j] for m in masks[h]]
        for place in range(len(masks[0])):
            for h in range(PARTS):
                mask = masks[h][place] ^ order[h][step]
                gather_cols(h, step, mask)
                note(mask)
                if place > 0 and 0 < h < PARTS - 1 and ready:
                    column(ready.pop(0))
            if place == 0 and ready:
                column(ready.pop(0))
            ready, finished = ready + finished, []
    for mask in ready + finished:
        column(mask)

    lead = jnp.transpose(jnp.broadcast_to(s_ref[c * n_row + r][0:1, :], (128, group)))[:, 0:1]
    lead = lead * (-32.0 / width)
    grads = []
    for h in range(PARTS):
        own = z_ref[h, own_rows, :].astype(jnp.float32)
        grads.append((lead * (sum_ref[...] * own - acc_ref[h])).astype(jnp.bfloat16))
    tile = 512
    for at in range(0, depth, tile):
        result = jnp.zeros((group, tile), jnp.float32)
        for h in range(PARTS):
            result += lax.dot_general(
                grads[h], w_ref[h, at : at + tile, :], NT_DIMS, preferred_element_type=jnp.float32
            )
        out_ref[:, at : at + tile] = result.astype(jnp.bfloat16)
    for copy in sends:
        copy.wait_send()
    for cond, copy in lines:
        pl.when(cond)(copy.wait_send)


def shards(features, w_proj, flags, rates):
    n_tensor, n_row, n_col = (lax.axis_size(name) for name in ("tensor", "row", "col"))
    group, depth = features.shape
    width = w_proj.shape[1]
    wide = width // PARTS
    quarter = group // n_tensor
    rows = group * n_row * n_col
    near = n_row * n_col - 1
    dma = pltpu.SemaphoreType.DMA
    return pl.pallas_call(
        functools.partial(kernel, n_tensor, n_row, n_col, rates.shape[0]),
        out_shape=jax.ShapeDtypeStruct((group, depth), jnp.bfloat16),
        in_specs=[
            pl.BlockSpec(memory_space=pltpu.HBM),
            pl.BlockSpec(memory_space=pltpu.HBM),
            pl.BlockSpec(memory_space=pltpu.VMEM),
            pl.BlockSpec(memory_space=pltpu.SMEM),
        ],
        out_specs=pl.BlockSpec(memory_space=pltpu.VMEM),
        scratch_shapes=[
            pltpu.VMEM((group, depth), jnp.bfloat16),
            pltpu.VMEM((PARTS, depth, wide), jnp.bfloat16),
            pltpu.VMEM((PARTS, group, wide), jnp.bfloat16),
            pltpu.VMEM((PARTS, n_tensor - 1, quarter, wide), jnp.bfloat16),
            pltpu.VMEM((PARTS, rows, wide), jnp.bfloat16),
            pltpu.VMEM((n_row * n_col, 8, group), jnp.float32),
            pltpu.VMEM((PARTS, group, wide), jnp.float32),
            pltpu.VMEM((group, 1), jnp.float32),
            dma((PARTS + 1,)),
            dma((PARTS, n_tensor - 1)),
            dma((PARTS, n_tensor - 1)),
            dma((PARTS, n_tensor, 2)),
            dma((PARTS, n_tensor - 1)),
            dma((PARTS, n_tensor, n_col)),
            dma((PARTS, n_tensor, n_col)),
            dma((PARTS, n_col, n_row - 1)),
            dma((PARTS, n_col, n_row - 1)),
            dma((near,)),
            dma((near,)),
        ],
        compiler_params=pltpu.CompilerParams(
            collective_id=0, has_side_effects=True, vmem_limit_bytes=56 * 1024 * 1024
        ),
        cost_estimate=pl.CostEstimate(
            flops=4 * group * depth * width + 4 * group * rows * width,
            bytes_accessed=2 * (depth * width + 2 * group * depth),
            transcendentals=rates.shape[0] * group * rows,
        ),
        name="mmd",
    )(features, w_proj, flags.reshape(1, group), rates)


def solution(mesh):
    in_specs = (P(("row", "col"), "tensor"), P("tensor", None), P(("row", "col")), P())
    out_specs = P(("row", "col"), "tensor")
    return jax.shard_map(shards, mesh=mesh, in_specs=in_specs, out_specs=out_specs, check_vma=False)
```

```python
import functools
import jax
import jax.numpy as jnp
from jax import lax
from jax.experimental import pallas as pl
from jax.experimental.pallas import tpu as pltpu
from jax.sharding import PartitionSpec as P

MESH = pl.DeviceIdType.MESH
PARTS = 2
NT_DIMS = (((1,), (1,)), ((), ()))


def kernel(
    n_tensor, n_row, n_col, n_rates,
    f_ref, w_hbm, flags_ref, rates_ref, out_ref,
    w_ref, part_ref, rs_ref, z_ref, s_ref, acc_ref, sum_ref,
    load_sem, rs_send, rs_recv, t_send, t_recv, c_send, c_recv, r_send, r_recv, s_send, s_recv,
):
    t, r, c = lax.axis_index("tensor"), lax.axis_index("row"), lax.axis_index("col")
    group = f_ref.shape[0]
    quarter = group // n_tensor
    depth, wide = w_ref.shape[1], w_ref.shape[2]
    width = wide * PARTS
    bits = [1 << b for b in range(n_col.bit_length() - 1)]
    order = [bits if h % 2 == 0 else bits[::-1] for h in range(PARTS)]
    runs = [(0, 1), (1, n_tensor)] if n_tensor > 1 else [(0, 1)]

    def slot(h, mask, dr, first=0, last=n_tensor):
        start = (mask * n_row + dr) * group
        return z_ref.at[h, start + first * quarter : start + last * quarter, :]

    sends = []

    def push(src, dst, send, recv, **to):
        copy = pltpu.make_async_remote_copy(
            src_ref=src, dst_ref=dst, send_sem=send, recv_sem=recv, device_id=to, device_id_type=MESH
        )
        copy.start()
        sends.append(copy)

    def arrived(dst, recv):
        pltpu.make_async_copy(dst, dst, recv).wait()

    loads = [
        pltpu.make_async_copy(w_hbm.at[:, h * wide : (h + 1) * wide], w_ref.at[h], load_sem.at[h])
        for h in range(PARTS)
    ]
    loads[0].start()

    barrier = pltpu.get_barrier_semaphore()
    near = [(dr, dc) for dr in range(n_row) for dc in range(n_col) if (dr, dc) != (0, 0)]
    for k in range(1, n_tensor):
        pl.semaphore_signal(
            barrier, inc=1, device_id={"tensor": lax.rem(t + k, n_tensor)}, device_id_type=MESH
        )
    for dr, mask in near:
        pl.semaphore_signal(
            barrier,
            inc=1,
            device_id={"row": lax.rem(r + dr, n_row), "col": jnp.bitwise_xor(c, mask)},
            device_id_type=MESH,
        )

    came = lax.broadcasted_iota(jnp.int32, (group, group), 0)
    goes = lax.broadcasted_iota(jnp.int32, (group, group), 1)
    goes = goes + t * quarter
    turn = (came == jnp.where(goes >= group, goes - group, goes)).astype(jnp.bfloat16)
    signs = jnp.broadcast_to((1 - 2 * flags_ref[...]).astype(jnp.float32), s_ref.shape[1:])
    s_ref[0] = jnp.dot(signs.astype(jnp.bfloat16), turn, preferred_element_type=jnp.float32)

    for h in range(PARTS):
        loads[h].wait()
        if h + 1 < PARTS:
            loads[h + 1].start()
        partial = jnp.dot(f_ref[...], w_ref[h], preferred_element_type=jnp.float32)
        part_ref[h] = partial.astype(jnp.bfloat16)
        acc_ref[h] = partial
        if h == 0:
            pl.semaphore_wait(barrier, n_tensor - 1 + len(near))
        for k in range(1, n_tensor):
            peer = lax.rem(t + k, n_tensor)
            rows = pl.ds(pl.multiple_of(peer * quarter, quarter), quarter)
            push(
                part_ref.at[h, rows, :], rs_ref.at[h, k - 1],
                rs_send.at[h, k - 1], rs_recv.at[h, k - 1], tensor=peer,
            )
    for index, (dr, mask) in enumerate(near):
        push(
            s_ref.at[0], s_ref.at[mask * n_row + dr], s_send.at[index], s_recv.at[index],
            row=lax.rem(r + dr, n_row), col=jnp.bitwise_xor(c, mask),
        )

    def to_cols(h, run, mask, step):
        for bit in order[h][step:]:
            push(
                slot(h, mask, 0, *runs[run]), slot(h, mask ^ bit, 0, *runs[run]),
                c_send.at[h, run, mask ^ bit], c_recv.at[h, run, mask ^ bit],
                col=jnp.bitwise_xor(c, bit),
            )

    def to_rows(h, mask):
        for dr in range(1, n_row):
            push(
                slot(h, mask, 0), slot(h, mask, dr),
                r_send.at[h, mask, dr - 1], r_recv.at[h, mask, dr - 1], row=lax.rem(r + dr, n_row),
            )

    def gather_cols(h, step, mask):
        for run in range(len(runs)):
            arrived(slot(h, mask, 0, *runs[run]), c_recv.at[h, run, mask])
            to_cols(h, run, mask, step + 1)
        to_rows(h, mask)

    for h in range(PARTS):
        total = acc_ref[h, pl.ds(pl.multiple_of(t * quarter, quarter), quarter), :]
        for k in range(1, n_tensor):
            arrived(rs_ref.at[h, k - 1], rs_recv.at[h, k - 1])
            total = total + rs_ref[h, k - 1].astype(jnp.float32)
        z_ref[h, 0:quarter, :] = total.astype(jnp.bfloat16)
        for k in range(1, n_tensor):
            push(
                slot(h, 0, 0, 0, 1), slot(h, 0, 0, k, k + 1), t_send.at[h, k - 1], t_recv.at[h, k - 1],
                tensor=lax.rem(t + n_tensor - k, n_tensor),
            )
        to_cols(h, 0, 0, 0)
    for h in range(PARTS):
        for k in range(1, n_tensor):
            arrived(slot(h, 0, 0, k, k + 1), t_recv.at[h, k - 1])
        if n_tensor > 1:
            to_cols(h, 1, 0, 0)
        to_rows(h, 0)

    acc_ref[...] = jnp.zeros_like(acc_ref)
    sum_ref[...] = jnp.zeros_like(sum_ref)
    for index, (dr, mask) in enumerate(near):
        arrived(s_ref.at[mask * n_row + dr], s_recv.at[index])

    own_norm = jnp.zeros((group, 1), jnp.float32)
    for h in range(PARTS):
        own_norm += jnp.sum(
            jnp.square(z_ref[h, 0:group, :].astype(jnp.float32)), axis=1, keepdims=True
        )

    def pairs(first, count):
        if isinstance(first, int):
            rows = slice(first * group, (first + count) * group)
        else:
            rows = pl.ds(pl.multiple_of(first * group, group), count * group)
        cross = jnp.zeros((group, count * group), jnp.float32)
        norm = jnp.zeros((count * group, 1), jnp.float32)
        for h in range(PARTS):
            other = z_ref[h, rows, :]
            norm += jnp.sum(jnp.square(other.astype(jnp.float32)), axis=1, keepdims=True)
            cross += lax.dot_general(
                z_ref[h, 0:group, :], other, NT_DIMS, preferred_element_type=jnp.float32
            )
        norm = jnp.transpose(jnp.broadcast_to(norm, (count * group, 128)))[0:1, :]
        sign = jnp.concatenate([s_ref[first + i][0:1, :] for i in range(count)], axis=1)
        dist = jnp.maximum(own_norm + norm - 2.0 * cross, 0.0) * (1.0 / width)
        mixed = jnp.zeros_like(dist)
        for band in range(n_rates):
            mixed = mixed + rates_ref[band] * jnp.exp(-rates_ref[band] * dist)
        mixed = mixed * sign
        sum_ref[...] += jnp.sum(mixed, axis=1, keepdims=True)
        rounded = mixed.astype(jnp.bfloat16)
        for h in range(PARTS):
            acc_ref[h] += jnp.dot(rounded, z_ref[h, rows, :], preferred_element_type=jnp.float32)

    def column(mask):
        for h in range(PARTS):
            for dr in range(1, n_row):
                arrived(slot(h, mask, dr), r_recv.at[h, mask, dr - 1])
        count = 2 if n_row % 2 == 0 else 1
        if n_row <= 2:
            pairs(mask * n_row, count)
        else:
            pl.loop(0, n_row // count)(lambda i: pairs(mask * n_row + i * count, count))

    have = {0: PARTS}
    ready, finished = [0], []
    for step in range(len(bits)):
        masks = [[0] for _ in range(PARTS)]
        for h in range(PARTS):
            for j in range(step):
                masks[h] = masks[h] + [m ^ order[h][j] for m in masks[h]]
        for place in range(len(masks[0])):
            for h in range(PARTS):
                mask = masks[h][place] ^ order[h][step]
                gather_cols(h, step, mask)
                have[mask] = have.get(mask, 0) + 1
                if have[mask] == PARTS:
                    finished.append(mask)
                if place > 0 and ready:
                    column(ready.pop(0))
            if step > 0 and place == 0 and ready:
                column(ready.pop(0))
            ready, finished = ready + finished, []
    for mask in ready + finished:
        column(mask)

    lead = jnp.transpose(jnp.broadcast_to(s_ref[0][0:1, :], (128, group)))[:, 0:1]
    lead = lead * (-32.0 / width)
    grads = []
    for h in range(PARTS):
        own = z_ref[h, 0:group, :].astype(jnp.float32)
        grads.append((lead * (sum_ref[...] * own - acc_ref[h])).astype(jnp.bfloat16))
    tile = 512
    for at in range(0, depth, tile):
        result = jnp.zeros((group, tile), jnp.float32)
        for h in range(PARTS):
            result += lax.dot_general(
                grads[h], w_ref[h, at : at + tile, :], NT_DIMS, preferred_element_type=jnp.float32
            )
        result = result.astype(jnp.bfloat16)
        for k in range(n_tensor):
            rows = pl.ds(pl.multiple_of(lax.rem(t + k, n_tensor) * quarter, quarter), quarter)
            out_ref[rows, at : at + tile] = result[k * quarter : (k + 1) * quarter]
    for copy in sends:
        copy.wait_send()


def shards(features, w_proj, flags, rates):
    n_tensor, n_row, n_col = (lax.axis_size(name) for name in ("tensor", "row", "col"))
    group, depth = features.shape
    width = w_proj.shape[1]
    wide = width // PARTS
    quarter = group // n_tensor
    rows = group * n_row * n_col
    near = n_row * n_col - 1
    dma = pltpu.SemaphoreType.DMA
    return pl.pallas_call(
        functools.partial(kernel, n_tensor, n_row, n_col, rates.shape[0]),
        out_shape=jax.ShapeDtypeStruct((group, depth), jnp.bfloat16),
        in_specs=[
            pl.BlockSpec(memory_space=pltpu.VMEM),
            pl.BlockSpec(memory_space=pltpu.HBM),
            pl.BlockSpec(memory_space=pltpu.VMEM),
            pl.BlockSpec(memory_space=pltpu.SMEM),
        ],
        out_specs=pl.BlockSpec(memory_space=pltpu.VMEM),
        scratch_shapes=[
            pltpu.VMEM((PARTS, depth, wide), jnp.bfloat16),
            pltpu.VMEM((PARTS, group, wide), jnp.bfloat16),
            pltpu.VMEM((PARTS, n_tensor - 1, quarter, wide), jnp.bfloat16),
            pltpu.VMEM((PARTS, rows, wide), jnp.bfloat16),
            pltpu.VMEM((n_row * n_col, 8, group), jnp.float32),
            pltpu.VMEM((PARTS, group, wide), jnp.float32),
            pltpu.VMEM((group, 1), jnp.float32),
            dma((PARTS,)),
            dma((PARTS, n_tensor - 1)),
            dma((PARTS, n_tensor - 1)),
            dma((PARTS, n_tensor - 1)),
            dma((PARTS, n_tensor - 1)),
            dma((PARTS, 2, n_col)),
            dma((PARTS, 2, n_col)),
            dma((PARTS, n_col, n_row - 1)),
            dma((PARTS, n_col, n_row - 1)),
            dma((near,)),
            dma((near,)),
        ],
        compiler_params=pltpu.CompilerParams(
            collective_id=0, has_side_effects=True, vmem_limit_bytes=52 * 1024 * 1024
        ),
        cost_estimate=pl.CostEstimate(
            flops=4 * group * depth * width + 4 * group * rows * width,
            bytes_accessed=2 * (depth * width + 2 * group * depth),
            transcendentals=rates.shape[0] * group * rows,
        ),
        name="mmd",
    )(features, w_proj, flags.reshape(1, group), rates)


def solution(mesh):
    in_specs = (P(("row", "col"), "tensor"), P("tensor", None), P(("row", "col")), P())
    out_specs = P(("row", "col"), "tensor")
    return jax.shard_map(shards, mesh=mesh, in_specs=in_specs, out_specs=out_specs, check_vma=False)
```

```python
import functools
import jax
import jax.numpy as jnp
from jax import lax
from jax.experimental import pallas as pl
from jax.experimental.pallas import tpu as pltpu
from jax.sharding import PartitionSpec as P

MESH = pl.DeviceIdType.MESH
PARTS = 2
NT_DIMS = (((1,), (1,)), ((), ()))


def kernel(
    n_tensor, n_row, n_col, n_rates,
    f_hbm, w_hbm, flags_ref, rates_ref, out_ref,
    f_ref, w_ref, part_ref, own_ref, rs_ref, z_ref, s_ref, acc_ref, sum_ref,
    load_sem, rs_send, rs_recv, t_send, t_recv, c_send, c_recv, r_send, r_recv, s_send, s_recv,
):
    t, r, c = lax.axis_index("tensor"), lax.axis_index("row"), lax.axis_index("col")
    group = f_ref.shape[0]
    quarter = group // n_tensor
    depth, wide = w_ref.shape[1], w_ref.shape[2]
    width = wide * PARTS
    bits = [1 << b for b in range(n_col.bit_length() - 1)]
    order = [bits if h % 2 == 0 else bits[::-1] for h in range(PARTS)]
    runs = [(0, 1), (1, n_tensor)] if n_tensor > 1 else [(0, 1)]

    def slot(h, mask, dr, first=0, last=n_tensor):
        start = (mask * n_row + dr) * group
        return z_ref.at[h, start + first * quarter : start + last * quarter, :]

    sends = []

    def push(src, dst, send, recv, **to):
        copy = pltpu.make_async_remote_copy(
            src_ref=src, dst_ref=dst, send_sem=send, recv_sem=recv, device_id=to, device_id_type=MESH
        )
        copy.start()
        sends.append(copy)

    def arrived(dst, recv):
        pltpu.make_async_copy(dst, dst, recv).wait()

    loads = [
        pltpu.make_async_copy(w_hbm.at[:, h * wide : (h + 1) * wide], w_ref.at[h], load_sem.at[h])
        for h in range(PARTS)
    ]
    loads.append(pltpu.make_async_copy(f_hbm, f_ref, load_sem.at[PARTS]))
    loads[PARTS].start()
    loads[0].start()

    barrier = pltpu.get_barrier_semaphore()
    near = [(dr, dc) for dr in range(n_row) for dc in range(n_col) if (dr, dc) != (0, 0)]
    for k in range(1, n_tensor):
        pl.semaphore_signal(
            barrier, inc=1, device_id={"tensor": lax.rem(t + k, n_tensor)}, device_id_type=MESH
        )
    for dr, mask in near:
        pl.semaphore_signal(
            barrier,
            inc=1,
            device_id={"row": lax.rem(r + dr, n_row), "col": jnp.bitwise_xor(c, mask)},
            device_id_type=MESH,
        )

    came = lax.broadcasted_iota(jnp.int32, (group, group), 0)
    goes = lax.broadcasted_iota(jnp.int32, (group, group), 1)
    goes = goes + t * quarter
    turn = (came == jnp.where(goes >= group, goes - group, goes)).astype(jnp.bfloat16)
    signs = jnp.broadcast_to((1 - 2 * flags_ref[...]).astype(jnp.float32), s_ref.shape[1:])
    s_ref[0] = jnp.dot(signs.astype(jnp.bfloat16), turn, preferred_element_type=jnp.float32)

    places = [0]
    halvings = n_tensor.bit_length() - 1
    for step in range(halvings):
        places = [2 * p for p in places] + [2 * p + 1 for p in places]

    def quarters(first, last):
        return slice(first * quarter, last * quarter)

    def halve(h, step):
        count = n_tensor >> (step + 1)
        push(
            part_ref.at[h, quarters(count, 2 * count), :], rs_ref.at[h, quarters(count, 2 * count), :],
            rs_send.at[h, step], rs_recv.at[h, step], tensor=jnp.bitwise_xor(t, 1 << step),
        )

    def halved(h, step):
        count = n_tensor >> (step + 1)
        landed = rs_ref.at[h, quarters(count, 2 * count), :]
        arrived(landed, rs_recv.at[h, step])
        total = acc_ref[h, quarters(0, count), :] + landed[...].astype(jnp.float32)
        if count == 1:
            z_ref[h, 0:quarter, :] = total.astype(jnp.bfloat16)
        else:
            half = count // 2 * quarter
            acc_ref[h, 0:half, :] = total[:half]
            part_ref[h, half : 2 * half, :] = total[half:].astype(jnp.bfloat16)
            halve(h, step + 1)

    loads[PARTS].wait()
    for h in range(PARTS):
        loads[h].wait()
        if h + 1 < PARTS:
            loads[h + 1].start()
        own_ref[...] = jnp.dot(f_ref[...], w_ref[h], preferred_element_type=jnp.float32)
        for index, place in enumerate(places):
            start = pl.multiple_of(jnp.bitwise_xor(t, place) * quarter, quarter)
            rows = own_ref[pl.ds(start, quarter), :]
            if 2 * index < n_tensor:
                acc_ref[h, quarters(index, index + 1), :] = rows
            else:
                part_ref[h, quarters(index, index + 1), :] = rows.astype(jnp.bfloat16)
        if h == 0:
            pl.semaphore_wait(barrier, n_tensor - 1 + len(near))
        halve(h, 0)
    for index, (dr, mask) in enumerate(near):
        push(
            s_ref.at[0], s_ref.at[mask * n_row + dr], s_send.at[index], s_recv.at[index],
            row=lax.rem(r + dr, n_row), col=jnp.bitwise_xor(c, mask),
        )

    def to_cols(h, run, mask, step):
        for bit in order[h][step:]:
            push(
                slot(h, mask, 0, *runs[run]), slot(h, mask ^ bit, 0, *runs[run]),
                c_send.at[h, run, mask ^ bit], c_recv.at[h, run, mask ^ bit],
                col=jnp.bitwise_xor(c, bit),
            )

    def to_rows(h, mask):
        for dr in range(1, n_row):
            push(
                slot(h, mask, 0), slot(h, mask, dr),
                r_send.at[h, mask, dr - 1], r_recv.at[h, mask, dr - 1], row=lax.rem(r + dr, n_row),
            )

    def gather_cols(h, step, mask):
        for run in range(len(runs)):
            arrived(slot(h, mask, 0, *runs[run]), c_recv.at[h, run, mask])
            to_cols(h, run, mask, step + 1)
        to_rows(h, mask)

    for step in range(halvings - 1):
        for h in range(PARTS):
            halved(h, step)
    for h in range(PARTS):
        halved(h, halvings - 1)
        for k in range(1, n_tensor):
            push(
                slot(h, 0, 0, 0, 1), slot(h, 0, 0, k, k + 1), t_send.at[h, k - 1], t_recv.at[h, k - 1],
                tensor=lax.rem(t + n_tensor - k, n_tensor),
            )
        to_cols(h, 0, 0, 0)
    for h in range(PARTS):
        for k in range(1, n_tensor):
            arrived(slot(h, 0, 0, k, k + 1), t_recv.at[h, k - 1])
        if n_tensor > 1:
            to_cols(h, 1, 0, 0)
        to_rows(h, 0)

    acc_ref[...] = jnp.zeros_like(acc_ref)
    sum_ref[...] = jnp.zeros_like(sum_ref)
    for index, (dr, mask) in enumerate(near):
        arrived(s_ref.at[mask * n_row + dr], s_recv.at[index])

    own_norm = jnp.zeros((group, 1), jnp.float32)
    for h in range(PARTS):
        own_norm += jnp.sum(
            jnp.square(z_ref[h, 0:group, :].astype(jnp.float32)), axis=1, keepdims=True
        )

    def pairs(first, count):
        if isinstance(first, int):
            rows = slice(first * group, (first + count) * group)
        else:
            rows = pl.ds(pl.multiple_of(first * group, group), count * group)
        cross = jnp.zeros((group, count * group), jnp.float32)
        norm = jnp.zeros((count * group, 1), jnp.float32)
        for h in range(PARTS):
            other = z_ref[h, rows, :]
            norm += jnp.sum(jnp.square(other.astype(jnp.float32)), axis=1, keepdims=True)
            cross += lax.dot_general(
                z_ref[h, 0:group, :], other, NT_DIMS, preferred_element_type=jnp.float32
            )
        norm = jnp.transpose(jnp.broadcast_to(norm, (count * group, 128)))[0:1, :]
        sign = jnp.concatenate([s_ref[first + i][0:1, :] for i in range(count)], axis=1)
        dist = jnp.maximum(own_norm + norm - 2.0 * cross, 0.0) * (1.0 / width)
        mixed = jnp.zeros_like(dist)
        for band in range(n_rates):
            mixed = mixed + rates_ref[band] * jnp.exp(-rates_ref[band] * dist)
        mixed = mixed * sign
        sum_ref[...] += jnp.sum(mixed, axis=1, keepdims=True)
        rounded = mixed.astype(jnp.bfloat16)
        for h in range(PARTS):
            acc_ref[h] += jnp.dot(rounded, z_ref[h, rows, :], preferred_element_type=jnp.float32)

    def column(mask):
        for h in range(PARTS):
            for dr in range(1, n_row):
                arrived(slot(h, mask, dr), r_recv.at[h, mask, dr - 1])
        count = 2 if n_row % 2 == 0 else 1
        if n_row <= 2:
            pairs(mask * n_row, count)
        else:
            pl.loop(0, n_row // count)(lambda i: pairs(mask * n_row + i * count, count))

    have = {0: PARTS}
    ready, finished = [0], []
    for step in range(len(bits)):
        masks = [[0] for _ in range(PARTS)]
        for h in range(PARTS):
            for j in range(step):
                masks[h] = masks[h] + [m ^ order[h][j] for m in masks[h]]
        for place in range(len(masks[0])):
            for h in range(PARTS):
                mask = masks[h][place] ^ order[h][step]
                gather_cols(h, step, mask)
                have[mask] = have.get(mask, 0) + 1
                if have[mask] == PARTS:
                    finished.append(mask)
                if place > 0 and ready:
                    column(ready.pop(0))
            if step > 0 and place == 0 and ready:
                column(ready.pop(0))
            ready, finished = ready + finished, []
    for mask in ready + finished:
        column(mask)

    lead = jnp.transpose(jnp.broadcast_to(s_ref[0][0:1, :], (128, group)))[:, 0:1]
    lead = lead * (-32.0 / width)
    grads = []
    for h in range(PARTS):
        own = z_ref[h, 0:group, :].astype(jnp.float32)
        grads.append((lead * (sum_ref[...] * own - acc_ref[h])).astype(jnp.bfloat16))
    for h in range(PARTS):
        for k in range(n_tensor):
            rows = pl.ds(pl.multiple_of(lax.rem(t + k, n_tensor) * quarter, quarter), quarter)
            out_ref[rows, h * wide : (h + 1) * wide] = grads[h][k * quarter : (k + 1) * quarter]
    for copy in sends:
        copy.wait_send()


def shards(features, w_proj, flags, rates):
    n_tensor, n_row, n_col = (lax.axis_size(name) for name in ("tensor", "row", "col"))
    group, depth = features.shape
    width = w_proj.shape[1]
    wide = width // PARTS
    quarter = group // n_tensor
    rows = group * n_row * n_col
    near = n_row * n_col - 1
    dma = pltpu.SemaphoreType.DMA
    grad_z = pl.pallas_call(
        functools.partial(kernel, n_tensor, n_row, n_col, rates.shape[0]),
        out_shape=jax.ShapeDtypeStruct((group, width), jnp.bfloat16),
        in_specs=[
            pl.BlockSpec(memory_space=pltpu.HBM),
            pl.BlockSpec(memory_space=pltpu.HBM),
            pl.BlockSpec(memory_space=pltpu.VMEM),
            pl.BlockSpec(memory_space=pltpu.SMEM),
        ],
        out_specs=pl.BlockSpec(memory_space=pltpu.VMEM),
        scratch_shapes=[
            pltpu.VMEM((group, depth), jnp.bfloat16),
            pltpu.VMEM((PARTS, depth, wide), jnp.bfloat16),
            pltpu.VMEM((PARTS, group, wide), jnp.bfloat16),
            pltpu.VMEM((group, wide), jnp.float32),
            pltpu.VMEM((PARTS, group, wide), jnp.bfloat16),
            pltpu.VMEM((PARTS, rows, wide), jnp.bfloat16),
            pltpu.VMEM((n_row * n_col, 8, group), jnp.float32),
            pltpu.VMEM((PARTS, group, wide), jnp.float32),
            pltpu.VMEM((group, 1), jnp.float32),
            dma((PARTS + 1,)),
            dma((PARTS, n_tensor - 1)),
            dma((PARTS, n_tensor - 1)),
            dma((PARTS, n_tensor - 1)),
            dma((PARTS, n_tensor - 1)),
            dma((PARTS, 2, n_col)),
            dma((PARTS, 2, n_col)),
            dma((PARTS, n_col, n_row - 1)),
            dma((PARTS, n_col, n_row - 1)),
            dma((near,)),
            dma((near,)),
        ],
        compiler_params=pltpu.CompilerParams(
            collective_id=0, has_side_effects=True, vmem_limit_bytes=56 * 1024 * 1024
        ),
        cost_estimate=pl.CostEstimate(
            flops=2 * group * depth * width + 4 * group * rows * width,
            bytes_accessed=2 * (depth * width + 2 * group * depth),
            transcendentals=rates.shape[0] * group * rows,
        ),
        name="mmd",
    )(features, w_proj, flags.reshape(1, group), rates)
    result = lax.dot_general(grad_z, w_proj, NT_DIMS, preferred_element_type=jnp.float32)
    return result.astype(jnp.bfloat16)


def solution(mesh):
    in_specs = (P(("row", "col"), "tensor"), P("tensor", None), P(("row", "col")), P())
    out_specs = P(("row", "col"), "tensor")
    return jax.shard_map(shards, mesh=mesh, in_specs=in_specs, out_specs=out_specs, check_vma=False)
```

```python
import functools
import jax
import jax.numpy as jnp
from jax import lax
from jax.experimental import pallas as pl
from jax.experimental.pallas import tpu as pltpu
from jax.sharding import PartitionSpec as P

MESH = pl.DeviceIdType.MESH
PARTS = 4
NT_DIMS = (((1,), (1,)), ((), ()))


def kernel(
    n_tensor, n_row, n_col, n_rates,
    f_hbm, w_hbm, flags_ref, rates_ref, out_ref,
    f_ref, w_ref, part_ref, own_ref, rs_ref, z_ref, s_ref, acc_ref, sum_ref,
    load_sem, rs_send, rs_recv, t_send, t_recv, c_send, c_recv, r_send, r_recv, s_send, s_recv,
):
    t, r, c = lax.axis_index("tensor"), lax.axis_index("row"), lax.axis_index("col")
    group = f_ref.shape[0]
    quarter = group // n_tensor
    depth, wide = w_ref.shape[1], w_ref.shape[2]
    width = wide * PARTS
    bits = [1 << b for b in range(n_col.bit_length() - 1)]
    order = [bits if h % 2 == 0 else bits[::-1] for h in range(PARTS)]
    runs = [(0, 1), (1, n_tensor)] if n_tensor > 1 else [(0, 1)]

    def slot(h, mask, dr, first=0, last=n_tensor):
        start = (mask * n_row + dr) * group
        return z_ref.at[h, start + first * quarter : start + last * quarter, :]

    sends = []

    def push(src, dst, send, recv, **to):
        copy = pltpu.make_async_remote_copy(
            src_ref=src, dst_ref=dst, send_sem=send, recv_sem=recv, device_id=to, device_id_type=MESH
        )
        copy.start()
        sends.append(copy)

    def arrived(dst, recv):
        pltpu.make_async_copy(dst, dst, recv).wait()

    loads = [
        pltpu.make_async_copy(w_hbm.at[:, h * wide : (h + 1) * wide], w_ref.at[h], load_sem.at[h])
        for h in range(PARTS)
    ]
    loads.append(pltpu.make_async_copy(f_hbm, f_ref, load_sem.at[PARTS]))
    loads[PARTS].start()
    loads[0].start()

    barrier = pltpu.get_barrier_semaphore()
    near = [(dr, dc) for dr in range(n_row) for dc in range(n_col) if (dr, dc) != (0, 0)]
    for k in range(1, n_tensor):
        pl.semaphore_signal(
            barrier, inc=1, device_id={"tensor": lax.rem(t + k, n_tensor)}, device_id_type=MESH
        )
    for dr, mask in near:
        pl.semaphore_signal(
            barrier,
            inc=1,
            device_id={"row": lax.rem(r + dr, n_row), "col": jnp.bitwise_xor(c, mask)},
            device_id_type=MESH,
        )

    came = lax.broadcasted_iota(jnp.int32, (group, group), 0)
    goes = lax.broadcasted_iota(jnp.int32, (group, group), 1)
    goes = goes + t * quarter
    turn = (came == jnp.where(goes >= group, goes - group, goes)).astype(jnp.bfloat16)
    signs = jnp.broadcast_to((1 - 2 * flags_ref[...]).astype(jnp.float32), s_ref.shape[1:])
    s_ref[0] = jnp.dot(signs.astype(jnp.bfloat16), turn, preferred_element_type=jnp.float32)

    places = [0]
    halvings = n_tensor.bit_length() - 1
    for step in range(halvings):
        places = [2 * p for p in places] + [2 * p + 1 for p in places]

    def quarters(first, last):
        return slice(first * quarter, last * quarter)

    def halve(h, step):
        count = n_tensor >> (step + 1)
        push(
            part_ref.at[h, quarters(count, 2 * count), :], rs_ref.at[h, quarters(count, 2 * count), :],
            rs_send.at[h, step], rs_recv.at[h, step], tensor=jnp.bitwise_xor(t, 1 << step),
        )

    def halved(h, step):
        count = n_tensor >> (step + 1)
        landed = rs_ref.at[h, quarters(count, 2 * count), :]
        arrived(landed, rs_recv.at[h, step])
        total = acc_ref[h, quarters(0, count), :] + landed[...].astype(jnp.float32)
        if count == 1:
            z_ref[h, 0:quarter, :] = total.astype(jnp.bfloat16)
        else:
            half = count // 2 * quarter
            acc_ref[h, 0:half, :] = total[:half]
            part_ref[h, half : 2 * half, :] = total[half:].astype(jnp.bfloat16)
            halve(h, step + 1)

    loads[PARTS].wait()
    for h in range(PARTS):
        loads[h].wait()
        if h + 1 < PARTS:
            loads[h + 1].start()
        own_ref[...] = jnp.dot(f_ref[...], w_ref[h], preferred_element_type=jnp.float32)
        for index, place in enumerate(places):
            start = pl.multiple_of(jnp.bitwise_xor(t, place) * quarter, quarter)
            rows = own_ref[pl.ds(start, quarter), :]
            if 2 * index < n_tensor:
                acc_ref[h, quarters(index, index + 1), :] = rows
            else:
                part_ref[h, quarters(index, index + 1), :] = rows.astype(jnp.bfloat16)
        if h == 0:
            pl.semaphore_wait(barrier, n_tensor - 1 + len(near))
        halve(h, 0)
    for index, (dr, mask) in enumerate(near):
        push(
            s_ref.at[0], s_ref.at[mask * n_row + dr], s_send.at[index], s_recv.at[index],
            row=lax.rem(r + dr, n_row), col=jnp.bitwise_xor(c, mask),
        )

    def to_cols(h, run, mask, step):
        for bit in order[h][step:]:
            push(
                slot(h, mask, 0, *runs[run]), slot(h, mask ^ bit, 0, *runs[run]),
                c_send.at[h, run, mask ^ bit], c_recv.at[h, run, mask ^ bit],
                col=jnp.bitwise_xor(c, bit),
            )

    def to_rows(h, mask):
        for dr in range(1, n_row):
            push(
                slot(h, mask, 0), slot(h, mask, dr),
                r_send.at[h, mask, dr - 1], r_recv.at[h, mask, dr - 1], row=lax.rem(r + dr, n_row),
            )

    def gather_cols(h, step, mask):
        for run in range(len(runs)):
            arrived(slot(h, mask, 0, *runs[run]), c_recv.at[h, run, mask])
            to_cols(h, run, mask, step + 1)
        to_rows(h, mask)

    def spread(h):
        for k in range(1, n_tensor):
            push(
                slot(h, 0, 0, 0, 1), slot(h, 0, 0, k, k + 1), t_send.at[h, k - 1], t_recv.at[h, k - 1],
                tensor=lax.rem(t + n_tensor - k, n_tensor),
            )
        to_cols(h, 0, 0, 0)

    for turn_at in range(PARTS + halvings - 1):
        for h in range(PARTS):
            step = turn_at - h
            if 0 <= step < halvings:
                halved(h, step)
                if step == halvings - 1:
                    spread(h)
    for h in range(PARTS):
        for k in range(1, n_tensor):
            arrived(slot(h, 0, 0, k, k + 1), t_recv.at[h, k - 1])
        if n_tensor > 1:
            to_cols(h, 1, 0, 0)
        to_rows(h, 0)

    acc_ref[...] = jnp.zeros_like(acc_ref)
    sum_ref[...] = jnp.zeros_like(sum_ref)
    for index, (dr, mask) in enumerate(near):
        arrived(s_ref.at[mask * n_row + dr], s_recv.at[index])

    own_norm = jnp.zeros((group, 1), jnp.float32)
    for h in range(PARTS):
        own_norm += jnp.sum(
            jnp.square(z_ref[h, 0:group, :].astype(jnp.float32)), axis=1, keepdims=True
        )

    def pairs(first, count):
        if isinstance(first, int):
            rows = slice(first * group, (first + count) * group)
        else:
            rows = pl.ds(pl.multiple_of(first * group, group), count * group)
        cross = jnp.zeros((group, count * group), jnp.float32)
        norm = jnp.zeros((count * group, 1), jnp.float32)
        for h in range(PARTS):
            other = z_ref[h, rows, :]
            norm += jnp.sum(jnp.square(other.astype(jnp.float32)), axis=1, keepdims=True)
            cross += lax.dot_general(
                z_ref[h, 0:group, :], other, NT_DIMS, preferred_element_type=jnp.float32
            )
        norm = jnp.transpose(jnp.broadcast_to(norm, (count * group, 128)))[0:1, :]
        sign = jnp.concatenate([s_ref[first + i][0:1, :] for i in range(count)], axis=1)
        dist = jnp.maximum(own_norm + norm - 2.0 * cross, 0.0) * (1.0 / width)
        mixed = jnp.zeros_like(dist)
        for band in range(n_rates):
            mixed = mixed + rates_ref[band] * jnp.exp(-rates_ref[band] * dist)
        mixed = mixed * sign
        sum_ref[...] += jnp.sum(mixed, axis=1, keepdims=True)
        rounded = mixed.astype(jnp.bfloat16)
        for h in range(PARTS):
            acc_ref[h] += jnp.dot(rounded, z_ref[h, rows, :], preferred_element_type=jnp.float32)

    def column(mask):
        for h in range(PARTS):
            for dr in range(1, n_row):
                arrived(slot(h, mask, dr), r_recv.at[h, mask, dr - 1])
        count = 2 if n_row % 2 == 0 else 1
        if n_row <= 2:
            pairs(mask * n_row, count)
        else:
            pl.loop(0, n_row // count)(lambda i: pairs(mask * n_row + i * count, count))

    have = {0: PARTS}
    ready, finished = [0], []
    for step in range(len(bits)):
        masks = [[0] for _ in range(PARTS)]
        for h in range(PARTS):
            for j in range(step):
                masks[h] = masks[h] + [m ^ order[h][j] for m in masks[h]]
        for place in range(len(masks[0])):
            for h in range(PARTS):
                mask = masks[h][place] ^ order[h][step]
                gather_cols(h, step, mask)
                have[mask] = have.get(mask, 0) + 1
                if have[mask] == PARTS:
                    finished.append(mask)
                if place > 0 and ready:
                    column(ready.pop(0))
            if step > 0 and place == 0 and ready:
                column(ready.pop(0))
            ready, finished = ready + finished, []
    for mask in ready + finished:
        column(mask)

    lead = jnp.transpose(jnp.broadcast_to(s_ref[0][0:1, :], (128, group)))[:, 0:1]
    lead = lead * (-32.0 / width)
    grads = []
    for h in range(PARTS):
        own = z_ref[h, 0:group, :].astype(jnp.float32)
        grads.append((lead * (sum_ref[...] * own - acc_ref[h])).astype(jnp.bfloat16))
    for h in range(PARTS):
        for k in range(n_tensor):
            rows = pl.ds(pl.multiple_of(lax.rem(t + k, n_tensor) * quarter, quarter), quarter)
            out_ref[rows, h * wide : (h + 1) * wide] = grads[h][k * quarter : (k + 1) * quarter]
    for copy in sends:
        copy.wait_send()


def shards(features, w_proj, flags, rates):
    n_tensor, n_row, n_col = (lax.axis_size(name) for name in ("tensor", "row", "col"))
    group, depth = features.shape
    width = w_proj.shape[1]
    wide = width // PARTS
    quarter = group // n_tensor
    rows = group * n_row * n_col
    near = n_row * n_col - 1
    dma = pltpu.SemaphoreType.DMA
    grad_z = pl.pallas_call(
        functools.partial(kernel, n_tensor, n_row, n_col, rates.shape[0]),
        out_shape=jax.ShapeDtypeStruct((group, width), jnp.bfloat16),
        in_specs=[
            pl.BlockSpec(memory_space=pltpu.HBM),
            pl.BlockSpec(memory_space=pltpu.HBM),
            pl.BlockSpec(memory_space=pltpu.VMEM),
            pl.BlockSpec(memory_space=pltpu.SMEM),
        ],
        out_specs=pl.BlockSpec(memory_space=pltpu.VMEM),
        scratch_shapes=[
            pltpu.VMEM((group, depth), jnp.bfloat16),
            pltpu.VMEM((PARTS, depth, wide), jnp.bfloat16),
            pltpu.VMEM((PARTS, group, wide), jnp.bfloat16),
            pltpu.VMEM((group, wide), jnp.float32),
            pltpu.VMEM((PARTS, group, wide), jnp.bfloat16),
            pltpu.VMEM((PARTS, rows, wide), jnp.bfloat16),
            pltpu.VMEM((n_row * n_col, 8, group), jnp.float32),
            pltpu.VMEM((PARTS, group, wide), jnp.float32),
            pltpu.VMEM((group, 1), jnp.float32),
            dma((PARTS + 1,)),
            dma((PARTS, n_tensor - 1)),
            dma((PARTS, n_tensor - 1)),
            dma((PARTS, n_tensor - 1)),
            dma((PARTS, n_tensor - 1)),
            dma((PARTS, 2, n_col)),
            dma((PARTS, 2, n_col)),
            dma((PARTS, n_col, n_row - 1)),
            dma((PARTS, n_col, n_row - 1)),
            dma((near,)),
            dma((near,)),
        ],
        compiler_params=pltpu.CompilerParams(
            collective_id=0, has_side_effects=True, vmem_limit_bytes=56 * 1024 * 1024
        ),
        cost_estimate=pl.CostEstimate(
            flops=2 * group * depth * width + 4 * group * rows * width,
            bytes_accessed=2 * (depth * width + 2 * group * depth),
            transcendentals=rates.shape[0] * group * rows,
        ),
        name="mmd",
    )(features, w_proj, flags.reshape(1, group), rates)
    result = lax.dot_general(grad_z, w_proj, NT_DIMS, preferred_element_type=jnp.float32)
    return result.astype(jnp.bfloat16)


def solution(mesh):
    in_specs = (P(("row", "col"), "tensor"), P("tensor", None), P(("row", "col")), P())
    out_specs = P(("row", "col"), "tensor")
    return jax.shard_map(shards, mesh=mesh, in_specs=in_specs, out_specs=out_specs, check_vma=False)
```

```python
import functools
import jax
import jax.numpy as jnp
from jax import lax
from jax.experimental import pallas as pl
from jax.experimental.pallas import tpu as pltpu
from jax.sharding import PartitionSpec as P

MESH = pl.DeviceIdType.MESH
PARTS = 2
NT_DIMS = (((1,), (1,)), ((), ()))


def kernel(
    n_tensor, n_row, n_col, n_rates,
    f_hbm, w_hbm, flags_ref, rates_ref, out_ref,
    f_ref, w_ref, part_ref, own_ref, rs_ref, z_ref, s_ref, acc_ref, sum_ref,
    load_sem, rs_send, rs_recv, t_send, t_recv, c_send, c_recv, r_send, r_recv, s_send, s_recv,
):
    t, r, c = lax.axis_index("tensor"), lax.axis_index("row"), lax.axis_index("col")
    group = f_ref.shape[0]
    quarter = group // n_tensor
    wide = w_ref.shape[2]
    width = wide * PARTS
    bits = [1 << b for b in range(n_col.bit_length() - 1)]
    runs = [(0, n_tensor // 2), (n_tensor // 2, n_tensor)]
    order = [bits, bits[::-1]]

    def blocks(mask, first, last):
        return z_ref.at[mask * group + first * quarter : mask * group + last * quarter, :]

    def layer(dr, first, last):
        return z_ref.at[(dr * n_col + first) * group : (dr * n_col + last) * group, :]

    sends = []

    def push(src, dst, send, recv, **to):
        copy = pltpu.make_async_remote_copy(
            src_ref=src, dst_ref=dst, send_sem=send, recv_sem=recv, device_id=to, device_id_type=MESH
        )
        copy.start()
        sends.append(copy)

    def arrived(dst, recv):
        pltpu.make_async_copy(dst, dst, recv).wait()

    loads = [
        pltpu.make_async_copy(w_hbm.at[:, h * wide : (h + 1) * wide], w_ref.at[h], load_sem.at[h])
        for h in range(PARTS)
    ]
    loads.append(pltpu.make_async_copy(f_hbm, f_ref, load_sem.at[PARTS]))
    loads[PARTS].start()
    loads[0].start()

    barrier = pltpu.get_barrier_semaphore()
    peers = [{"tensor": lax.rem(t + k, n_tensor)} for k in range(1, n_tensor)]
    peers += [{"row": lax.rem(r + dr, n_row)} for dr in range(1, n_row)]
    peers += [{"col": jnp.bitwise_xor(c, bit)} for bit in bits]
    for peer in peers:
        pl.semaphore_signal(barrier, inc=1, device_id=peer, device_id_type=MESH)

    came = lax.broadcasted_iota(jnp.int32, (group, group), 0)
    goes = lax.broadcasted_iota(jnp.int32, (group, group), 1)
    goes = goes + t * quarter
    turn = (came == jnp.where(goes >= group, goes - group, goes)).astype(jnp.bfloat16)
    signs = jnp.broadcast_to((1 - 2 * flags_ref[...]).astype(jnp.float32), s_ref.shape[1:])
    s_ref[0] = jnp.dot(signs.astype(jnp.bfloat16), turn, preferred_element_type=jnp.float32)

    loads[PARTS].wait()
    for h in range(PARTS):
        loads[h].wait()
        if h + 1 < PARTS:
            loads[h + 1].start()
        partial = jnp.dot(f_ref[...], w_ref[h], preferred_element_type=jnp.float32)
        part_ref[h] = partial.astype(jnp.bfloat16)
        own_ref[h] = partial
        if h == 0:
            pl.semaphore_wait(barrier, len(peers))
        for k in range(1, n_tensor):
            peer = lax.rem(t + k, n_tensor)
            rows = pl.ds(pl.multiple_of(peer * quarter, quarter), quarter)
            push(
                part_ref.at[h, rows, :], rs_ref.at[h, k - 1],
                rs_send.at[h, k - 1], rs_recv.at[h, k - 1], tensor=peer,
            )

    for index, bit in enumerate(bits):
        push(
            s_ref.at[0:bit], s_ref.at[bit : 2 * bit], s_send.at[index], s_recv.at[index],
            col=jnp.bitwise_xor(c, bit),
        )
        arrived(s_ref.at[bit : 2 * bit], s_recv.at[index])
    for dr in range(1, n_row):
        index = len(bits) + dr - 1
        push(
            s_ref.at[0:n_col], s_ref.at[dr * n_col : (dr + 1) * n_col], s_send.at[index], s_recv.at[index],
            row=lax.rem(r + dr, n_row),
        )
    acc_ref[...] = jnp.zeros_like(acc_ref)
    sum_ref[...] = jnp.zeros_like(sum_ref)

    for h in range(PARTS):
        total = own_ref[h, pl.ds(pl.multiple_of(t * quarter, quarter), quarter), :]
        for k in range(1, n_tensor):
            arrived(rs_ref.at[h, k - 1], rs_recv.at[h, k - 1])
            total = total + rs_ref[h, k - 1].astype(jnp.float32)
        z_ref[0:quarter, h * wide : (h + 1) * wide] = total.astype(jnp.bfloat16)
    for k in range(1, n_tensor):
        push(
            blocks(0, 0, 1), blocks(0, k, k + 1), t_send.at[k - 1], t_recv.at[k - 1],
            tensor=lax.rem(t + n_tensor - k, n_tensor),
        )

    def to_cols(run, mask, step):
        for bit in order[run][step:]:
            push(
                blocks(mask, *runs[run]), blocks(mask ^ bit, *runs[run]),
                c_send.at[run, mask ^ bit], c_recv.at[run, mask ^ bit], col=jnp.bitwise_xor(c, bit),
            )

    for run, (first, last) in enumerate(runs):
        for k in range(max(first, 1), last):
            arrived(blocks(0, k, k + 1), t_recv.at[k - 1])
        to_cols(run, 0, 0)

    own_norm = jnp.sum(jnp.square(z_ref[0:group, :].astype(jnp.float32)), axis=1, keepdims=True)

    def pairs(first, count):
        if isinstance(first, int):
            rows = slice(first * group, (first + count) * group)
        else:
            rows = pl.ds(pl.multiple_of(first * group, group), count * group)
        other = z_ref[rows, :]
        norm = jnp.sum(jnp.square(other.astype(jnp.float32)), axis=1, keepdims=True)
        cross = lax.dot_general(
            z_ref[0:group, :], other, NT_DIMS, preferred_element_type=jnp.float32
        )
        norm = jnp.transpose(jnp.broadcast_to(norm, (count * group, 128)))[0:1, :]
        sign = jnp.concatenate([s_ref[first + i][0:1, :] for i in range(count)], axis=1)
        dist = jnp.maximum(own_norm + norm - 2.0 * cross, 0.0) * (1.0 / width)
        mixed = jnp.zeros_like(dist)
        for band in range(n_rates):
            mixed = mixed + rates_ref[band] * jnp.exp(-rates_ref[band] * dist)
        mixed = mixed * sign
        sum_ref[...] += jnp.sum(mixed, axis=1, keepdims=True)
        acc_ref[...] += jnp.dot(
            mixed.astype(jnp.bfloat16), z_ref[rows, :], preferred_element_type=jnp.float32
        )

    def most(dr):
        count = (n_col - 2) // 2
        if count > 1:
            pl.loop(0, count)(lambda i: pairs(dr * n_col + 2 * i, 2))
        else:
            pairs(dr * n_col, 2)

    def to_rows(part, first, last):
        for dr in range(1, n_row):
            push(
                layer(0, first, last), layer(dr, first, last),
                r_send.at[part, dr - 1], r_recv.at[part, dr - 1], row=lax.rem(r + dr, n_row),
            )

    for step in range(len(bits)):
        masks = [[0], [0]]
        for run in range(2):
            for j in range(step):
                masks[run] = masks[run] + [m ^ order[run][j] for m in masks[run]]
        for place in range(len(masks[0])):
            if step == len(bits) - 1 and place == len(masks[0]) - 1:
                to_rows(0, 0, n_col - 1)
                for index in range(len(bits), len(bits) + n_row - 1):
                    dr = index - len(bits) + 1
                    arrived(s_ref.at[dr * n_col : (dr + 1) * n_col], s_recv.at[index])
                most(0)
                for dr in range(1, n_row):
                    arrived(layer(dr, 0, n_col - 1), r_recv.at[0, dr - 1])
                    most(dr)
            for run in range(2):
                mask = masks[run][place] ^ order[run][step]
                arrived(blocks(mask, *runs[run]), c_recv.at[run, mask])
                to_cols(run, mask, step + 1)
    to_rows(1, n_col - 1, n_col)
    pairs(n_col - 2, 2)
    for dr in range(1, n_row):
        arrived(layer(dr, n_col - 1, n_col), r_recv.at[1, dr - 1])
        pairs(dr * n_col + n_col - 2, 2)

    lead = jnp.transpose(jnp.broadcast_to(s_ref[0][0:1, :], (128, group)))[:, 0:1]
    lead = lead * (-32.0 / width)
    own = z_ref[0:group, :].astype(jnp.float32)
    grads = (lead * (sum_ref[...] * own - acc_ref[...])).astype(jnp.bfloat16)
    for k in range(n_tensor):
        rows = pl.ds(pl.multiple_of(lax.rem(t + k, n_tensor) * quarter, quarter), quarter)
        out_ref[rows, :] = grads[k * quarter : (k + 1) * quarter]
    for copy in sends:
        copy.wait_send()


def shards(features, w_proj, flags, rates):
    n_tensor, n_row, n_col = (lax.axis_size(name) for name in ("tensor", "row", "col"))
    group, depth = features.shape
    width = w_proj.shape[1]
    wide = width // PARTS
    quarter = group // n_tensor
    rows = group * n_row * n_col
    hops = n_col.bit_length() - 1 + n_row - 1
    dma = pltpu.SemaphoreType.DMA
    grad_z = pl.pallas_call(
        functools.partial(kernel, n_tensor, n_row, n_col, rates.shape[0]),
        out_shape=jax.ShapeDtypeStruct((group, width), jnp.bfloat16),
        in_specs=[
            pl.BlockSpec(memory_space=pltpu.HBM),
            pl.BlockSpec(memory_space=pltpu.HBM),
            pl.BlockSpec(memory_space=pltpu.VMEM),
            pl.BlockSpec(memory_space=pltpu.SMEM),
        ],
        out_specs=pl.BlockSpec(memory_space=pltpu.VMEM),
        scratch_shapes=[
            pltpu.VMEM((group, depth), jnp.bfloat16),
            pltpu.VMEM((PARTS, depth, wide), jnp.bfloat16),
            pltpu.VMEM((PARTS, group, wide), jnp.bfloat16),
            pltpu.VMEM((PARTS, group, wide), jnp.float32),
            pltpu.VMEM((PARTS, n_tensor - 1, quarter, wide), jnp.bfloat16),
            pltpu.VMEM((rows, width), jnp.bfloat16),
            pltpu.VMEM((n_row * n_col, 8, group), jnp.float32),
            pltpu.VMEM((group, width), jnp.float32),
            pltpu.VMEM((group, 1), jnp.float32),
            dma((PARTS + 1,)),
            dma((PARTS, n_tensor - 1)),
            dma((PARTS, n_tensor - 1)),
            dma((n_tensor - 1,)),
            dma((n_tensor - 1,)),
            dma((2, n_col)),
            dma((2, n_col)),
            dma((2, n_row - 1)),
            dma((2, n_row - 1)),
            dma((hops,)),
            dma((hops,)),
        ],
        compiler_params=pltpu.CompilerParams(
            collective_id=0, has_side_effects=True, vmem_limit_bytes=56 * 1024 * 1024
        ),
        cost_estimate=pl.CostEstimate(
            flops=2 * group * depth * width + 4 * group * rows * width,
            bytes_accessed=2 * (depth * width + 2 * group * depth),
            transcendentals=rates.shape[0] * group * rows,
        ),
        name="mmd",
    )(features, w_proj, flags.reshape(1, group), rates)
    result = lax.dot_general(grad_z, w_proj, NT_DIMS, preferred_element_type=jnp.float32)
    return result.astype(jnp.bfloat16)


def solution(mesh):
    in_specs = (P(("row", "col"), "tensor"), P("tensor", None), P(("row", "col")), P())
    out_specs = P(("row", "col"), "tensor")
    return jax.shard_map(shards, mesh=mesh, in_specs=in_specs, out_specs=out_specs, check_vma=False)
```

```python
import functools
import jax
import jax.numpy as jnp
from jax import lax
from jax.experimental import pallas as pl
from jax.experimental.pallas import tpu as pltpu
from jax.sharding import PartitionSpec as P

MESH = pl.DeviceIdType.MESH
PARTS = 2
NT_DIMS = (((1,), (1,)), ((), ()))


def kernel(
    n_tensor, n_row, n_col, n_rates,
    f_hbm, w_hbm, flags_ref, rates_ref, out_ref,
    f_ref, w_ref, part_ref, rs_ref, z_ref, s_ref, acc_ref, sum_ref,
    load_sem, rs_send, rs_recv, t_send, t_recv, c_send, c_recv, r_send, r_recv, s_send, s_recv,
):
    t, r, c = lax.axis_index("tensor"), lax.axis_index("row"), lax.axis_index("col")
    group = f_ref.shape[0]
    quarter = group // n_tensor
    depth, wide = w_ref.shape[1], w_ref.shape[2]
    width = wide * PARTS
    bits = [1 << b for b in range(n_col.bit_length() - 1)]
    order = [bits if h % 2 == 0 else bits[::-1] for h in range(PARTS)]
    runs = [(0, 1), (1, n_tensor)] if n_tensor > 1 else [(0, 1)]

    def slot(h, mask, dr, first=0, last=n_tensor):
        start = (mask * n_row + dr) * group
        return z_ref.at[h, start + first * quarter : start + last * quarter, :]

    sends = []

    def push(src, dst, send, recv, **to):
        copy = pltpu.make_async_remote_copy(
            src_ref=src, dst_ref=dst, send_sem=send, recv_sem=recv, device_id=to, device_id_type=MESH
        )
        copy.start()
        sends.append(copy)

    def arrived(dst, recv):
        pltpu.make_async_copy(dst, dst, recv).wait()

    loads = [
        pltpu.make_async_copy(w_hbm.at[:, h * wide : (h + 1) * wide], w_ref.at[h], load_sem.at[h])
        for h in range(PARTS)
    ]
    loads.append(pltpu.make_async_copy(f_hbm, f_ref, load_sem.at[PARTS]))
    loads[PARTS].start()
    loads[0].start()

    barrier = pltpu.get_barrier_semaphore()
    peers = [{"tensor": lax.rem(t + k, n_tensor)} for k in range(1, n_tensor)]
    peers += [{"row": lax.rem(r + dr, n_row)} for dr in range(1, n_row)]
    peers += [{"col": jnp.bitwise_xor(c, bit)} for bit in bits]
    for peer in peers:
        pl.semaphore_signal(barrier, inc=1, device_id=peer, device_id_type=MESH)

    came = lax.broadcasted_iota(jnp.int32, (group, group), 0)
    goes = lax.broadcasted_iota(jnp.int32, (group, group), 1)
    goes = goes + t * quarter
    turn = (came == jnp.where(goes >= group, goes - group, goes)).astype(jnp.bfloat16)
    signs = jnp.broadcast_to((1 - 2 * flags_ref[...]).astype(jnp.float32), s_ref.shape[1:])
    s_ref[0] = jnp.dot(signs.astype(jnp.bfloat16), turn, preferred_element_type=jnp.float32)

    loads[PARTS].wait()
    for h in range(PARTS):
        loads[h].wait()
        if h + 1 < PARTS:
            loads[h + 1].start()
        partial = jnp.dot(f_ref[...], w_ref[h], preferred_element_type=jnp.float32)
        part_ref[h] = partial.astype(jnp.bfloat16)
        acc_ref[h] = partial
        if h == 0:
            pl.semaphore_wait(barrier, len(peers))
        for k in range(1, n_tensor):
            peer = lax.rem(t + k, n_tensor)
            rows = pl.ds(pl.multiple_of(peer * quarter, quarter), quarter)
            push(
                part_ref.at[h, rows, :], rs_ref.at[h, k - 1],
                rs_send.at[h, k - 1], rs_recv.at[h, k - 1], tensor=peer,
            )
    hops = [({"row": lax.rem(r + dr, n_row)}, 0, dr, 1) for dr in range(1, n_row)]
    hops += [({"col": jnp.bitwise_xor(c, bit)}, 0, bit * n_row, bit * n_row) for bit in bits]
    for index, (to, src, dst, count) in enumerate(hops):
        landed = s_ref.at[dst : dst + count]
        push(s_ref.at[src : src + count], landed, s_send.at[index], s_recv.at[index], **to)
        if index >= n_row - 2 and index + 1 < len(hops):
            for before in range(index + 1 if index == n_row - 2 else 0):
                arrived(s_ref.at[hops[before][2] : hops[before][2] + 1], s_recv.at[before])
            if index > n_row - 2:
                arrived(landed, s_recv.at[index])

    def to_cols(h, run, mask, step):
        for bit in order[h][step:]:
            push(
                slot(h, mask, 0, *runs[run]), slot(h, mask ^ bit, 0, *runs[run]),
                c_send.at[h, run, mask ^ bit], c_recv.at[h, run, mask ^ bit],
                col=jnp.bitwise_xor(c, bit),
            )

    def to_rows(h, mask):
        for dr in range(1, n_row):
            push(
                slot(h, mask, 0), slot(h, mask, dr),
                r_send.at[h, mask, dr - 1], r_recv.at[h, mask, dr - 1], row=lax.rem(r + dr, n_row),
            )

    def gather_cols(h, step, mask):
        for run in range(len(runs)):
            arrived(slot(h, mask, 0, *runs[run]), c_recv.at[h, run, mask])
            to_cols(h, run, mask, step + 1)
        to_rows(h, mask)

    for h in range(PARTS):
        total = acc_ref[h, pl.ds(pl.multiple_of(t * quarter, quarter), quarter), :]
        for k in range(1, n_tensor):
            arrived(rs_ref.at[h, k - 1], rs_recv.at[h, k - 1])
            total = total + rs_ref[h, k - 1].astype(jnp.float32)
        z_ref[h, 0:quarter, :] = total.astype(jnp.bfloat16)
        for k in range(1, n_tensor):
            push(
                slot(h, 0, 0, 0, 1), slot(h, 0, 0, k, k + 1), t_send.at[h, k - 1], t_recv.at[h, k - 1],
                tensor=lax.rem(t + n_tensor - k, n_tensor),
            )
        to_cols(h, 0, 0, 0)
    for h in range(PARTS):
        for k in range(1, n_tensor):
            arrived(slot(h, 0, 0, k, k + 1), t_recv.at[h, k - 1])
        if n_tensor > 1:
            to_cols(h, 1, 0, 0)
        to_rows(h, 0)

    acc_ref[...] = jnp.zeros_like(acc_ref)
    sum_ref[...] = jnp.zeros_like(sum_ref)
    last = hops[-1]
    arrived(s_ref.at[last[2] : last[2] + last[3]], s_recv.at[len(hops) - 1])

    own_norm = jnp.zeros((group, 1), jnp.float32)
    for h in range(PARTS):
        own_norm += jnp.sum(
            jnp.square(z_ref[h, 0:group, :].astype(jnp.float32)), axis=1, keepdims=True
        )

    def pairs(first, count):
        if isinstance(first, int):
            rows = slice(first * group, (first + count) * group)
        else:
            rows = pl.ds(pl.multiple_of(first * group, group), count * group)
        cross = jnp.zeros((group, count * group), jnp.float32)
        norm = jnp.zeros((count * group, 1), jnp.float32)
        for h in range(PARTS):
            other = z_ref[h, rows, :]
            norm += jnp.sum(jnp.square(other.astype(jnp.float32)), axis=1, keepdims=True)
            cross += lax.dot_general(
                z_ref[h, 0:group, :], other, NT_DIMS, preferred_element_type=jnp.float32
            )
        norm = jnp.transpose(jnp.broadcast_to(norm, (count * group, 128)))[0:1, :]
        sign = jnp.concatenate([s_ref[first + i][0:1, :] for i in range(count)], axis=1)
        dist = jnp.maximum(own_norm + norm - 2.0 * cross, 0.0) * (1.0 / width)
        mixed = jnp.zeros_like(dist)
        for band in range(n_rates):
            mixed = mixed + rates_ref[band] * jnp.exp(-rates_ref[band] * dist)
        mixed = mixed * sign
        sum_ref[...] += jnp.sum(mixed, axis=1, keepdims=True)
        rounded = mixed.astype(jnp.bfloat16)
        for h in range(PARTS):
            acc_ref[h] += jnp.dot(rounded, z_ref[h, rows, :], preferred_element_type=jnp.float32)

    def column(mask):
        for h in range(PARTS):
            for dr in range(1, n_row):
                arrived(slot(h, mask, dr), r_recv.at[h, mask, dr - 1])
        count = 2 if n_row % 2 == 0 else 1
        if n_row <= 2:
            pairs(mask * n_row, count)
        else:
            pl.loop(0, n_row // count)(lambda i: pairs(mask * n_row + i * count, count))

    have = {0: PARTS}
    ready, finished = [0], []
    for step in range(len(bits)):
        masks = [[0] for _ in range(PARTS)]
        for h in range(PARTS):
            for j in range(step):
                masks[h] = masks[h] + [m ^ order[h][j] for m in masks[h]]
        for place in range(len(masks[0])):
            for h in range(PARTS):
                mask = masks[h][place] ^ order[h][step]
                gather_cols(h, step, mask)
                have[mask] = have.get(mask, 0) + 1
                if have[mask] == PARTS:
                    finished.append(mask)
                if place > 0 and ready:
                    column(ready.pop(0))
            if step > 0 and place == 0 and ready:
                column(ready.pop(0))
            ready, finished = ready + finished, []
    for mask in ready + finished:
        if mask == n_col - 1:
            for copy in sends:
                copy.wait_send()
        column(mask)

    lead = jnp.transpose(jnp.broadcast_to(s_ref[0][0:1, :], (128, group)))[:, 0:1]
    lead = lead * (-32.0 / width)
    grads = []
    for h in range(PARTS):
        own = z_ref[h, 0:group, :].astype(jnp.float32)
        grads.append((lead * (sum_ref[...] * own - acc_ref[h])).astype(jnp.bfloat16))
    for h in range(PARTS):
        for k in range(n_tensor):
            rows = pl.ds(pl.multiple_of(lax.rem(t + k, n_tensor) * quarter, quarter), quarter)
            out_ref[rows, h * wide : (h + 1) * wide] = grads[h][k * quarter : (k + 1) * quarter]


def shards(features, w_proj, flags, rates):
    n_tensor, n_row, n_col = (lax.axis_size(name) for name in ("tensor", "row", "col"))
    group, depth = features.shape
    width = w_proj.shape[1]
    wide = width // PARTS
    quarter = group // n_tensor
    rows = group * n_row * n_col
    near = n_row - 1 + n_col.bit_length() - 1
    dma = pltpu.SemaphoreType.DMA
    grad_z = pl.pallas_call(
        functools.partial(kernel, n_tensor, n_row, n_col, rates.shape[0]),
        out_shape=jax.ShapeDtypeStruct((group, width), jnp.bfloat16),
        in_specs=[
            pl.BlockSpec(memory_space=pltpu.HBM),
            pl.BlockSpec(memory_space=pltpu.HBM),
            pl.BlockSpec(memory_space=pltpu.VMEM),
            pl.BlockSpec(memory_space=pltpu.SMEM),
        ],
        out_specs=pl.BlockSpec(memory_space=pltpu.VMEM),
        scratch_shapes=[
            pltpu.VMEM((group, depth), jnp.bfloat16),
            pltpu.VMEM((PARTS, depth, wide), jnp.bfloat16),
            pltpu.VMEM((PARTS, group, wide), jnp.bfloat16),
            pltpu.VMEM((PARTS, n_tensor - 1, quarter, wide), jnp.bfloat16),
            pltpu.VMEM((PARTS, rows, wide), jnp.bfloat16),
            pltpu.VMEM((n_row * n_col, 8, group), jnp.float32),
            pltpu.VMEM((PARTS, group, wide), jnp.float32),
            pltpu.VMEM((group, 1), jnp.float32),
            dma((PARTS + 1,)),
            dma((PARTS, n_tensor - 1)),
            dma((PARTS, n_tensor - 1)),
            dma((PARTS, n_tensor - 1)),
            dma((PARTS, n_tensor - 1)),
            dma((PARTS, 2, n_col)),
            dma((PARTS, 2, n_col)),
            dma((PARTS, n_col, n_row - 1)),
            dma((PARTS, n_col, n_row - 1)),
            dma((near,)),
            dma((near,)),
        ],
        compiler_params=pltpu.CompilerParams(
            collective_id=0, has_side_effects=True, vmem_limit_bytes=56 * 1024 * 1024
        ),
        cost_estimate=pl.CostEstimate(
            flops=2 * group * depth * width + 4 * group * rows * width,
            bytes_accessed=2 * (depth * width + 2 * group * depth),
            transcendentals=rates.shape[0] * group * rows,
        ),
        name="mmd",
    )(features, w_proj, flags.reshape(1, group), rates)
    result = lax.dot_general(grad_z, w_proj, NT_DIMS, preferred_element_type=jnp.float32)
    return result.astype(jnp.bfloat16)


def solution(mesh):
    in_specs = (P(("row", "col"), "tensor"), P("tensor", None), P(("row", "col")), P())
    out_specs = P(("row", "col"), "tensor")
    return jax.shard_map(shards, mesh=mesh, in_specs=in_specs, out_specs=out_specs, check_vma=False)
```

```python
import functools
import jax
import jax.numpy as jnp
from jax import lax
from jax.experimental import pallas as pl
from jax.experimental.pallas import tpu as pltpu
from jax.sharding import PartitionSpec as P

MESH = pl.DeviceIdType.MESH
PARTS = 2
NT_DIMS = (((1,), (1,)), ((), ()))


def kernel(
    n_tensor, n_row, n_col, n_rates,
    f_hbm, w_hbm, flags_ref, rates_ref, out_ref,
    f_ref, w_ref, part_ref, rs_ref, z_ref, s_ref, acc_ref, sum_ref,
    load_sem, rs_send, rs_recv, t_send, t_recv, c_send, c_recv, r_send, r_recv, s_send, s_recv,
):
    t, r, c = lax.axis_index("tensor"), lax.axis_index("row"), lax.axis_index("col")
    group = f_ref.shape[0]
    quarter = group // n_tensor
    depth, wide = w_ref.shape[1], w_ref.shape[2]
    width = wide * PARTS
    bits = [1 << b for b in range(n_col.bit_length() - 1)]
    order = [bits if h % 2 == 0 else bits[::-1] for h in range(PARTS)]
    runs = [(0, 1), (1, n_tensor)] if n_tensor > 1 else [(0, 1)]

    def slot(h, mask, dr, first=0, last=n_tensor):
        start = (mask * n_row + dr) * group
        return z_ref.at[h, start + first * quarter : start + last * quarter, :]

    sends = []

    def push(src, dst, send, recv, **to):
        copy = pltpu.make_async_remote_copy(
            src_ref=src, dst_ref=dst, send_sem=send, recv_sem=recv, device_id=to, device_id_type=MESH
        )
        copy.start()
        sends.append(copy)

    def arrived(dst, recv):
        pltpu.make_async_copy(dst, dst, recv).wait()

    loads = [
        pltpu.make_async_copy(w_hbm.at[:, h * wide : (h + 1) * wide], w_ref.at[h], load_sem.at[h])
        for h in range(PARTS)
    ]
    loads.append(pltpu.make_async_copy(f_hbm, f_ref, load_sem.at[PARTS]))
    loads[PARTS].start()
    loads[0].start()

    barrier = pltpu.get_barrier_semaphore()
    peers = [{"tensor": lax.rem(t + k, n_tensor)} for k in range(1, n_tensor)]
    peers += [{"row": lax.rem(r + dr, n_row)} for dr in range(1, n_row)]
    peers += [{"col": jnp.bitwise_xor(c, bit)} for bit in bits]
    for peer in peers:
        pl.semaphore_signal(barrier, inc=1, device_id=peer, device_id_type=MESH)

    came = lax.broadcasted_iota(jnp.int32, (group, group), 0)
    goes = lax.broadcasted_iota(jnp.int32, (group, group), 1)
    goes = goes + t * quarter
    turn = (came == jnp.where(goes >= group, goes - group, goes)).astype(jnp.bfloat16)
    signs = jnp.broadcast_to((1 - 2 * flags_ref[...]).astype(jnp.float32), s_ref.shape[1:])
    s_ref[0] = jnp.dot(signs.astype(jnp.bfloat16), turn, preferred_element_type=jnp.float32)

    loads[PARTS].wait()
    for h in range(PARTS):
        loads[h].wait()
        if h + 1 < PARTS:
            loads[h + 1].start()
        partial = jnp.dot(f_ref[...], w_ref[h], preferred_element_type=jnp.float32)
        part_ref[h] = partial.astype(jnp.bfloat16)
        acc_ref[h] = partial
        if h == 0:
            pl.semaphore_wait(barrier, len(peers))
        for k in range(1, n_tensor):
            peer = lax.rem(t + k, n_tensor)
            rows = pl.ds(pl.multiple_of(peer * quarter, quarter), quarter)
            push(
                part_ref.at[h, rows, :], rs_ref.at[h, k - 1],
                rs_send.at[h, k - 1], rs_recv.at[h, k - 1], tensor=peer,
            )
    hops = [({"row": lax.rem(r + dr, n_row)}, 0, dr, 1) for dr in range(1, n_row)]
    hops += [({"col": jnp.bitwise_xor(c, bit)}, 0, bit * n_row, bit * n_row) for bit in bits]
    for index, (to, src, dst, count) in enumerate(hops):
        landed = s_ref.at[dst : dst + count]
        push(s_ref.at[src : src + count], landed, s_send.at[index], s_recv.at[index], **to)
        if index >= n_row - 2 and index + 1 < len(hops):
            for before in range(index + 1 if index == n_row - 2 else 0):
                arrived(s_ref.at[hops[before][2] : hops[before][2] + 1], s_recv.at[before])
            if index > n_row - 2:
                arrived(landed, s_recv.at[index])

    def to_cols(h, run, mask, step):
        for bit in order[h][step:]:
            push(
                slot(h, mask, 0, *runs[run]), slot(h, mask ^ bit, 0, *runs[run]),
                c_send.at[h, run, mask ^ bit], c_recv.at[h, run, mask ^ bit],
                col=jnp.bitwise_xor(c, bit),
            )

    def to_rows(h, mask):
        for dr in range(1, n_row):
            push(
                slot(h, mask, 0), slot(h, mask, dr),
                r_send.at[h, mask, dr - 1], r_recv.at[h, mask, dr - 1], row=lax.rem(r + dr, n_row),
            )

    def gather_cols(h, step, mask):
        for run in range(len(runs)):
            arrived(slot(h, mask, 0, *runs[run]), c_recv.at[h, run, mask])
            to_cols(h, run, mask, step + 1)
        to_rows(h, mask)

    for h in range(PARTS):
        total = acc_ref[h, pl.ds(pl.multiple_of(t * quarter, quarter), quarter), :]
        for k in range(1, n_tensor):
            arrived(rs_ref.at[h, k - 1], rs_recv.at[h, k - 1])
            total = total + rs_ref[h, k - 1].astype(jnp.float32)
        z_ref[h, 0:quarter, :] = total.astype(jnp.bfloat16)
        for k in range(1, n_tensor):
            push(
                slot(h, 0, 0, 0, 1), slot(h, 0, 0, k, k + 1), t_send.at[h, k - 1], t_recv.at[h, k - 1],
                tensor=lax.rem(t + n_tensor - k, n_tensor),
            )
        to_cols(h, 0, 0, 0)
    for h in range(PARTS):
        for k in range(1, n_tensor):
            arrived(slot(h, 0, 0, k, k + 1), t_recv.at[h, k - 1])
        if n_tensor > 1:
            to_cols(h, 1, 0, 0)
        to_rows(h, 0)

    acc_ref[...] = jnp.zeros_like(acc_ref)
    sum_ref[...] = jnp.zeros_like(sum_ref)
    last = hops[-1]
    arrived(s_ref.at[last[2] : last[2] + last[3]], s_recv.at[len(hops) - 1])

    own_norm = jnp.zeros((group, 1), jnp.float32)
    for h in range(PARTS):
        own_norm += jnp.sum(
            jnp.square(z_ref[h, 0:group, :].astype(jnp.float32)), axis=1, keepdims=True
        )

    def pairs(first, count):
        if isinstance(first, int):
            rows = slice(first * group, (first + count) * group)
        else:
            rows = pl.ds(pl.multiple_of(first * group, group), count * group)
        cross = jnp.zeros((group, count * group), jnp.float32)
        norm = jnp.zeros((count * group, 1), jnp.float32)
        for h in range(PARTS):
            other = z_ref[h, rows, :]
            norm += jnp.sum(jnp.square(other.astype(jnp.float32)), axis=1, keepdims=True)
            cross += lax.dot_general(
                z_ref[h, 0:group, :], other, NT_DIMS, preferred_element_type=jnp.float32
            )
        norm = jnp.transpose(jnp.broadcast_to(norm, (count * group, 128)))[0:1, :]
        sign = jnp.concatenate([s_ref[first + i][0:1, :] for i in range(count)], axis=1)
        dist = jnp.maximum(own_norm + norm - 2.0 * cross, 0.0) * (1.0 / width)
        mixed = jnp.zeros_like(dist)
        for band in range(n_rates):
            mixed = mixed + rates_ref[band] * jnp.exp(-rates_ref[band] * dist)
        mixed = mixed * sign
        sum_ref[...] += jnp.sum(mixed, axis=1, keepdims=True)
        rounded = mixed.astype(jnp.bfloat16)
        for h in range(PARTS):
            acc_ref[h] += jnp.dot(rounded, z_ref[h, rows, :], preferred_element_type=jnp.float32)

    def column(mask):
        for h in range(PARTS):
            for dr in range(1, n_row):
                arrived(slot(h, mask, dr), r_recv.at[h, mask, dr - 1])
        count = 2 if n_row % 2 == 0 else 1
        if n_row <= 2:
            pairs(mask * n_row, count)
        else:
            pl.loop(0, n_row // count)(lambda i: pairs(mask * n_row + i * count, count))

    have = {0: PARTS}
    ready, finished = [0], []
    for step in range(len(bits)):
        masks = [[0] for _ in range(PARTS)]
        for h in range(PARTS):
            for j in range(step):
                masks[h] = masks[h] + [m ^ order[h][j] for m in masks[h]]
        for place in range(len(masks[0])):
            for h in range(PARTS):
                mask = masks[h][place] ^ order[h][step]
                gather_cols(h, step, mask)
                have[mask] = have.get(mask, 0) + 1
                if have[mask] == PARTS:
                    finished.append(mask)
                if place > 0 and ready:
                    column(ready.pop(0))
            if step > 0 and place == 0 and ready:
                column(ready.pop(0))
            ready, finished = ready + finished, []
    for mask in ready + finished:
        if mask == n_col - 1:
            for copy in sends:
                copy.wait_send()
        column(mask)

    lead = jnp.transpose(jnp.broadcast_to(s_ref[0][0:1, :], (128, group)))[:, 0:1]
    lead = lead * (-32.0 / width)
    grads = []
    for h in range(PARTS):
        own = z_ref[h, 0:group, :].astype(jnp.float32)
        grads.append((lead * (sum_ref[...] * own - acc_ref[h])).astype(jnp.bfloat16))
    for h in range(PARTS):
        for k in range(n_tensor):
            rows = pl.ds(pl.multiple_of(lax.rem(t + k, n_tensor) * quarter, quarter), quarter)
            out_ref[rows, h * wide : (h + 1) * wide] = grads[h][k * quarter : (k + 1) * quarter]


def product(grad_ref, w_ref, out_ref):
    tile = 512
    for at in range(0, out_ref.shape[1], tile):
        out_ref[:, at : at + tile] = lax.dot_general(
            grad_ref[...], w_ref[at : at + tile, :], NT_DIMS, preferred_element_type=jnp.float32
        ).astype(jnp.bfloat16)


def shards(features, w_proj, flags, rates):
    n_tensor, n_row, n_col = (lax.axis_size(name) for name in ("tensor", "row", "col"))
    group, depth = features.shape
    width = w_proj.shape[1]
    wide = width // PARTS
    quarter = group // n_tensor
    rows = group * n_row * n_col
    near = n_row - 1 + n_col.bit_length() - 1
    dma = pltpu.SemaphoreType.DMA
    grad_z = pl.pallas_call(
        functools.partial(kernel, n_tensor, n_row, n_col, rates.shape[0]),
        out_shape=jax.ShapeDtypeStruct((group, width), jnp.bfloat16),
        in_specs=[
            pl.BlockSpec(memory_space=pltpu.HBM),
            pl.BlockSpec(memory_space=pltpu.HBM),
            pl.BlockSpec(memory_space=pltpu.VMEM),
            pl.BlockSpec(memory_space=pltpu.SMEM),
        ],
        out_specs=pl.BlockSpec(memory_space=pltpu.VMEM),
        scratch_shapes=[
            pltpu.VMEM((group, depth), jnp.bfloat16),
            pltpu.VMEM((PARTS, depth, wide), jnp.bfloat16),
            pltpu.VMEM((PARTS, group, wide), jnp.bfloat16),
            pltpu.VMEM((PARTS, n_tensor - 1, quarter, wide), jnp.bfloat16),
            pltpu.VMEM((PARTS, rows, wide), jnp.bfloat16),
            pltpu.VMEM((n_row * n_col, 8, group), jnp.float32),
            pltpu.VMEM((PARTS, group, wide), jnp.float32),
            pltpu.VMEM((group, 1), jnp.float32),
            dma((PARTS + 1,)),
            dma((PARTS, n_tensor - 1)),
            dma((PARTS, n_tensor - 1)),
            dma((PARTS, n_tensor - 1)),
            dma((PARTS, n_tensor - 1)),
            dma((PARTS, 2, n_col)),
            dma((PARTS, 2, n_col)),
            dma((PARTS, n_col, n_row - 1)),
            dma((PARTS, n_col, n_row - 1)),
            dma((near,)),
            dma((near,)),
        ],
        compiler_params=pltpu.CompilerParams(
            collective_id=0, has_side_effects=True, vmem_limit_bytes=56 * 1024 * 1024
        ),
        cost_estimate=pl.CostEstimate(
            flops=2 * group * depth * width + 4 * group * rows * width,
            bytes_accessed=2 * (depth * width + 2 * group * depth),
            transcendentals=rates.shape[0] * group * rows,
        ),
        name="mmd",
    )(features, w_proj, flags.reshape(1, group), rates)
    return pl.pallas_call(
        product,
        out_shape=jax.ShapeDtypeStruct((group, depth), jnp.bfloat16),
        in_specs=[pl.BlockSpec(memory_space=pltpu.VMEM)] * 2,
        out_specs=pl.BlockSpec(memory_space=pltpu.VMEM),
        compiler_params=pltpu.CompilerParams(vmem_limit_bytes=16 * 1024 * 1024),
        cost_estimate=pl.CostEstimate(
            flops=2 * group * depth * width,
            bytes_accessed=2 * (depth * width + group * (depth + width)),
            transcendentals=0,
        ),
        name="product",
    )(grad_z, w_proj)


def solution(mesh):
    in_specs = (P(("row", "col"), "tensor"), P("tensor", None), P(("row", "col")), P())
    out_specs = P(("row", "col"), "tensor")
    return jax.shard_map(shards, mesh=mesh, in_specs=in_specs, out_specs=out_specs, check_vma=False)
```
